32 devices in a mesh: seq: 8 (over z, y), head: 4 (over x, core).
Axes of the slice: x: 2, y: 2, z: 4, core: 2. Of those that a mesh axis runs over, the one named last changes fastest.
Arguments:
- x_in: bfloat16 [2, 2048, 2048], P(None, ('seq', 'head')), may hold values from -6 to 6
- lengths: int32 [2, 3], replicated, may hold values from 128 to 1792, as said below
- cotangent: bfloat16 [2, 2048, 2048], P(None, ('seq', 'head')), may hold values from -6 to 6
- w_in: float32 [2048, 8512], P(('seq', 'head')), may hold values from -0.125 to 0.125
- m_in: float32 [2048, 8512], P(('seq', 'head')), may hold values from -112 to 112
- v_in: float32 [2048, 8512], P(('seq', 'head')), may hold values from 163.84 to 655.36
- w_out: float32 [4096, 2048], P(('seq', 'head')), may hold values from -0.09375 to 0.09375
- m_out: float32 [4096, 2048], P(('seq', 'head')), may hold values from -384 to 384
- v_out: float32 [4096, 2048], P(('seq', 'head')), may hold values from 1761.28 to 6963.2
- conv_w: float32 [4352, 4], P(('seq', 'head')), may hold values from -3 to 3
- m_conv: float32 [4352, 4], P(('seq', 'head')), may hold values from -112 to 112
- v_conv: float32 [4352, 4], P(('seq', 'head')), may hold values from 163.84 to 655.36
- vectors: float32 [10496], P(('seq', 'head')), may hold values from -0.9 to 1.7
- m_vec: float32 [10496], P(('seq', 'head')), may hold values from -256 to 256
- v_vec: float32 [10496], P(('seq', 'head')), may hold values from 819.2 to 3481.6
- head_params: float32 [3, 64], P(None, 'head'), may hold values from -13.2 to 8
- m_head: float32 [3, 64], P(None, 'head'), may hold values from -768 to 768
- v_head: float32 [3, 64], P(None, 'head'), may hold values from 6963.2 to 28672
Outputs:
- layer_out: bfloat16 [2, 2048, 2048], P(None, ('seq', 'head'))
- input_grad: bfloat16 [2, 2048, 2048], P(None, ('seq', 'head'))
- w_in_new: float32 [2048, 8512], P(('seq', 'head'))
- m_in_new: float32 [2048, 8512], P(('seq', 'head'))
- v_in_new: float32 [2048, 8512], P(('seq', 'head'))
- w_out_new: float32 [4096, 2048], P(('seq', 'head'))
- m_out_new: float32 [4096, 2048], P(('seq', 'head'))
- v_out_new: float32 [4096, 2048], P(('seq', 'head'))
- conv_new: float32 [4352, 4], P(('seq', 'head'))
- m_conv_new: float32 [4352, 4], P(('seq', 'head'))
- v_conv_new: float32 [4352, 4], P(('seq', 'head'))
- vec_new: float32 [10496], P(('seq', 'head'))
- m_vec_new: float32 [10496], P(('seq', 'head'))
- v_vec_new: float32 [10496], P(('seq', 'head'))
- head_new: float32 [3, 64], P(None, 'head')
- m_head_new: float32 [3, 64], P(None, 'head')
- v_head_new: float32 [3, 64], P(None, 'head')
The draws below stay inside these ranges and needn't reach their ends.
Inputs may be any that keep to these rules, and one draw needn't show every extreme that they name: In each group the first and the last sequence hold at least 128 and fewer than 256 tokens, the middle one the rest; a group's lengths sum to 2048; in one group both the first and the last hold exactly 128.
All inputs are finite; a program needn't handle non-finite values.
Results may differ from the reference program's by a relative error of at most 0.01.
The reference program's roundings to bfloat16 on the way count: a program that leaves them out, or rounds other values in their place, can miss the bound.
Values may be sent and summed in bfloat16 or wider, within the bound.
No kernel may reach another device: no remote copies, remote signals or barrier semaphores. Data moves between devices by JAX's collectives and lax.ppermute only.
A program may use at most 384 MiB of HBM per device.

```python
import math
import jax
import jax.numpy as jnp
from jax import lax

D = 2048
HEADS = 64
HEAD_DIM = 64
STATE = 128
KW = 4
BLOCK = 256
GROUPS = 2
STEP = 4
INNER = 4096
CONV = 4352
PROJ = 8512
VEC = 10496
SPAN = 256
GROUP_TOK = 2048


def draw_lengths(key, part):
    key = jax.random.fold_in(key, 5)
    first_key, last_key, pick_key = jax.random.split(key, 3)
    first_len = jax.random.randint(first_key, (GROUPS,), SPAN // 2, SPAN)
    last_len = jax.random.randint(last_key, (GROUPS,), SPAN // 2, SPAN)
    chosen = jax.random.randint(pick_key, (), 0, GROUPS)
    picked = jnp.arange(GROUPS) == chosen
    first_len = jnp.where(picked, SPAN // 2, first_len)
    last_len = jnp.where(picked, SPAN // 2, last_len)
    middle_len = GROUP_TOK - first_len - last_len
    return jnp.stack([first_len, middle_len, last_len], axis=1).astype(jnp.int32)


def draw_vectors(key, part):
    key = jax.random.fold_in(key, 7)
    gain_key, bias_key, gate_key = jax.random.split(key, 3)
    lower, upper = (0.5, 1.5)
    norm_gain = jax.random.uniform(gain_key, (D,), jnp.float32, lower, upper)
    conv_bias = 0.3 * jnp.clip(jax.random.normal(bias_key, (CONV,), jnp.float32), -3.0, 3.0)
    gate_gain = jax.random.uniform(gate_key, (INNER,), jnp.float32, lower, upper)
    return jnp.concatenate([norm_gain, conv_bias, gate_gain]).astype(jnp.float32)


def draw_head_params(key, part):
    key = jax.random.fold_in(key, 9)
    bias_key, rate_key, skip_key = jax.random.split(key, 3)
    lower = math.log(0.05 / GROUP_TOK)
    upper = math.log(0.1)
    dt_bias = jax.random.uniform(bias_key, (HEADS,), jnp.float32, -1.5, 0.5)
    a_log = jax.random.uniform(rate_key, (HEADS,), jnp.float32, lower, upper)
    skip = jax.random.uniform(skip_key, (HEADS,), jnp.float32, 2.0, 8.0)
    return jnp.stack([dt_bias, a_log, skip]).astype(jnp.float32)


def level_of(own_key, shape, cuts, smallest, largest):
    gain, own = 1.0, jax.random.fold_in(own_key, 6)
    for dim, blocks in cuts:
        draws = jnp.exp(jax.random.uniform(jax.random.fold_in(own, dim), (blocks,), jnp.float32, smallest / len(cuts), largest / len(cuts)))
        gain = gain * jnp.repeat(draws, shape[dim] // blocks).reshape([-1 if axis == dim else 1 for axis in range(len(shape))])
    return gain


def bell_draw(own_key, extent, width, bound, cuts=(), kind=jnp.bfloat16):
    gain = level_of(own_key, extent, cuts, -0.22, 0.18) if cuts else 1.0
    drawn = jax.random.normal(own_key, extent, jnp.float32) * width * gain
    return jnp.minimum(jnp.maximum(drawn, -bound), bound).astype(kind)


def setup_inputs(seed: int = 0) -> dict:
    streams_of = jax.random.split(jax.random.key(seed), 19)
    return {
        "x_in": bell_draw(streams_of[0], (GROUPS, GROUP_TOK, D), 1.0, 6.0, ((1, 32),)),
        "lengths": draw_lengths(jax.random.fold_in(streams_of[18], 71), 0),
        "cotangent": bell_draw(streams_of[2], (GROUPS, GROUP_TOK, D), 1.0, 6.0, ((1, 32),)),
        "w_in": bell_draw(streams_of[3], (D, PROJ), D ** -0.5, 0.125, ((0, 32),), jnp.float32),
        "m_in": bell_draw(streams_of[4], (D, PROJ), (0.3 * (GROUPS * GROUP_TOK) ** 0.5), 112.0, ((0, 32),), jnp.float32),
        "v_in": jnp.clip(jnp.exp(math.log(655.36) - 1.3862944 * jax.random.uniform(streams_of[5], (D, PROJ), jnp.float32) ** level_of(streams_of[5], (D, PROJ), ((0, 32),), -0.2, 0.2)), 163.84, 655.36),
        "w_out": bell_draw(streams_of[6], (INNER, D), INNER ** -0.5, 0.09375, ((0, 32),), jnp.float32),
        "m_out": bell_draw(streams_of[7], (INNER, D), ((GROUPS * GROUP_TOK) ** 0.5), 384.0, ((0, 32),), jnp.float32),
        "v_out": jnp.clip(jnp.exp(math.log(6963.2) - 1.37459833 * jax.random.uniform(streams_of[8], (INNER, D), jnp.float32) ** level_of(streams_of[8], (INNER, D), ((0, 32),), -0.2, 0.2)), 1761.28, 6963.2),
        "conv_w": bell_draw(streams_of[9], (CONV, KW), KW ** -0.5, 3.0, ((0, 32),), jnp.float32),
        "m_conv": bell_draw(streams_of[10], (CONV, KW), (0.3 * (GROUPS * GROUP_TOK) ** 0.5), 112.0, ((0, 32),), jnp.float32),
        "v_conv": jnp.clip(jnp.exp(math.log(655.36) - 1.3862944 * jax.random.uniform(streams_of[11], (CONV, KW), jnp.float32) ** level_of(streams_of[11], (CONV, KW), ((0, 32),), -0.2, 0.2)), 163.84, 655.36),
        "vectors": draw_vectors(jax.random.fold_in(streams_of[18], 71), 0),
        "m_vec": bell_draw(streams_of[13], (VEC,), (0.7 * (GROUPS * GROUP_TOK) ** 0.5), 256.0, ((0, 32),), jnp.float32),
        "v_vec": jnp.clip(jnp.exp(math.log(3481.6) - 1.446919 * jax.random.uniform(streams_of[14], (VEC,), jnp.float32) ** level_of(streams_of[14], (VEC,), ((0, 32),), -0.2, 0.2)), 819.2, 3481.6),
        "head_params": draw_head_params(jax.random.fold_in(streams_of[18], 71), 0),
        "m_head": bell_draw(streams_of[16], (3, HEADS), (2.0 * (GROUPS * GROUP_TOK) ** 0.5), 768.0, ((1, 4),), jnp.float32),
        "v_head": jnp.clip(jnp.exp(math.log(28672.0) - 1.4152819 * jax.random.uniform(streams_of[17], (3, HEADS), jnp.float32) ** level_of(streams_of[17], (3, HEADS), ((1, 4),), -0.2, 0.2)), 6963.2, 28672.0),
    }


EPS = 1e-05
BETA_ONE = 0.5
BETA_TWO = 0.7
ADAM_EPS = 1e-08
DECAY = 0.1
rate_input = 0.02
rate_output = 0.015
rate_conv = 0.3
rate_vector = 0.5
rate_head = 0.5
HIGH = lax.Precision.HIGHEST

@jax.custom_vjp
def low(v):
    return lax.optimization_barrier(v.astype(jnp.bfloat16)).astype(jnp.float32)

@jax.custom_vjp
def low_back(v):
    return v

def low_keep(v):
    return (low(v), None)

def low_pass(kept, grad):
    return (grad,)

def back_keep(v):
    return (v, None)

def back_low(kept, grad):
    return (low(grad),)
low.defvjp(low_keep, low_pass)
low_back.defvjp(back_keep, back_low)

def start_flags(length_row, first_pos, count):
    offsets = (jnp.cumsum(length_row) - length_row).astype(jnp.int32)
    places = (first_pos + jnp.arange(count)).astype(jnp.int32)
    return jnp.any(places[:, None] == offsets[None, :], axis=1).astype(jnp.int32)

def conv_mix(extended, taps, shift_term, start_ext):
    tok_span = extended.shape[0] - (KW - 1)
    counts = jnp.cumsum(start_ext)
    total = shift_term[None, :] + taps[:, KW - 1][None, :] * extended[KW - 1:]
    for tap in range(KW - 1):
        lag = KW - 1 - tap
        valid = counts[KW - 1:] - counts[KW - 1 - lag:KW - 1 - lag + tok_span] == 0
        total = total + taps[:, tap][None, :] * extended[tap:tap + tok_span] * valid[:, None].astype(extended.dtype)
    return total

def block_step(memory, block):
    values, key_rows, query_rows, step_size, log_decay, starts = block
    running = jnp.cumsum(log_decay, axis=0)
    segment = jnp.cumsum(starts)
    places = jnp.arange(starts.shape[0])
    within = (segment[:, None] == segment[None, :]) & (places[:, None] >= places[None, :])
    gaps = running[:, None, :] - running[None, :, :]
    decays = jnp.exp(jnp.where(within[:, :, None], gaps, 0.0)) * within[:, :, None].astype(log_decay.dtype)
    scores = jnp.dot(query_rows, key_rows.T, precision=HIGH)
    weighted = values * step_size[:, :, None]
    output_h = jnp.einsum('tsh,shp->thp', scores[:, :, None] * decays, weighted, precision=HIGH)
    inflow = jnp.exp(running) * (segment == 0).astype(log_decay.dtype)[:, None]
    output_h = output_h + jnp.einsum('tn,hpn->thp', query_rows, memory, precision=HIGH) * inflow[:, :, None]
    to_end = jnp.exp(running[-1][None, :] - running) * (segment == segment[-1]).astype(log_decay.dtype)[:, None]
    carried = jnp.exp(running[-1]) * (segment[-1] == 0).astype(log_decay.dtype)
    memory = carried[:, None, None] * memory + jnp.einsum('sh,shp,sn->hpn', to_end, weighted, key_rows, precision=HIGH)
    return (memory, output_h)

def ssd_run(values, key_rows, query_rows, step_size, log_decay, starts):
    blocks = values.shape[0] // BLOCK

    def blocked(array):
        return array.reshape((blocks, BLOCK) + array.shape[1:])
    memory = jnp.zeros((values.shape[1], values.shape[2], key_rows.shape[1]), values.dtype)
    memory, outputs = lax.scan(jax.checkpoint(block_step), memory, (blocked(values), blocked(key_rows), blocked(query_rows), blocked(step_size), blocked(log_decay), blocked(starts)))
    return (outputs.reshape(values.shape), memory)

def layer_group(x_group, start_ext, w_in_b, w_out_b, taps_b, vec_b, head_terms):
    norm_gain = vec_b[:D]
    conv_bias = vec_b[D:D + CONV]
    gate_gain = vec_b[D + CONV:]
    scale = lax.rsqrt(lax.optimization_barrier(jnp.mean(x_group * x_group, axis=-1, keepdims=True)) + EPS)
    normed = low(x_group * scale * norm_gain)
    proj = low_back(jnp.dot(normed, w_in_b, precision=HIGH))
    gate_in = proj[:, :INNER]
    mixer = low(proj[:, INNER:INNER + CONV])
    step_raw = low(proj[:, INNER + CONV:])
    extended = jnp.concatenate([jnp.zeros((KW - 1, CONV), x_group.dtype), mixer], 0)
    act = jax.nn.silu(conv_mix(extended, taps_b, conv_bias, start_ext))
    values = act[:, :INNER].reshape(-1, HEADS, HEAD_DIM)
    key_rows = act[:, INNER:INNER + STATE]
    query_rows = act[:, INNER + STATE:]
    step_size = jax.nn.softplus(step_raw + head_terms[0])
    log_decay = -jnp.exp(head_terms[1]) * step_size
    scanned, unused = ssd_run(values, key_rows, query_rows, step_size, log_decay, start_ext[KW - 1:])
    scanned = scanned + head_terms[2][None, :, None] * values
    scan_out = low_back(low(scanned.reshape(-1, INNER)))
    gated = scan_out * jax.nn.silu(gate_in)
    gnorm = low(gated * lax.rsqrt(lax.optimization_barrier(jnp.mean(gated * gated, axis=-1, keepdims=True)) + EPS) * gate_gain)
    return x_group + jnp.dot(gnorm, w_out_b, precision=HIGH)

def adam(weight, first, second, grad, rate):
    first_new = BETA_ONE * first + (1.0 - BETA_ONE) * grad
    second_new = BETA_TWO * second + (1.0 - BETA_TWO) * grad * grad
    update = first_new / (1.0 - BETA_ONE ** STEP) / (jnp.sqrt(second_new / (1.0 - BETA_TWO ** STEP)) + ADAM_EPS)
    return (weight - rate * (update + DECAY * weight), first_new, second_new)

def reference(x_in, lengths, cotangent, w_in, m_in, v_in, w_out, m_out, v_out, conv_w, m_conv, v_conv, vectors, m_vec, v_vec, head_params, m_head, v_head):
    starts = jax.vmap(lambda length_row: start_flags(length_row, -(KW - 1), GROUP_TOK + KW - 1))(lengths)

    def forward(x_float, w_in_f, w_out_f, taps_f, vec_f, head_terms):
        w_in_b = low(w_in_f)
        w_out_b = low(w_out_f)
        taps_b = low(taps_f)
        vec_b = low(vec_f)

        def one_group(pair):
            return layer_group(pair[0], pair[1], w_in_b, w_out_b, taps_b, vec_b, head_terms)
        return lax.map(jax.checkpoint(one_group), (x_float, starts))
    x_float = x_in.astype(jnp.float32)
    outputs, pull = jax.vjp(forward, x_float, w_in, w_out, conv_w, vectors, head_params)
    grad_x, grad_in, grad_out, grad_conv, grad_vec, grad_head = pull(cotangent.astype(jnp.float32))
    input_grad = grad_x.astype(jnp.bfloat16)
    in_new = adam(w_in, m_in, v_in, grad_in, rate_input)
    out_new = adam(w_out, m_out, v_out, grad_out, rate_output)
    conv_new = adam(conv_w, m_conv, v_conv, grad_conv, rate_conv)
    vec_new = adam(vectors, m_vec, v_vec, grad_vec, rate_vector)
    head_new = adam(head_params, m_head, v_head, grad_head, rate_head)
    return (outputs.astype(jnp.bfloat16), input_grad, in_new[0], in_new[1], in_new[2], out_new[0], out_new[1], out_new[2], conv_new[0], conv_new[1], conv_new[2], vec_new[0], vec_new[1], vec_new[2], head_new[0], head_new[1], head_new[2])
```

```python
import functools

import jax
import jax.numpy as jnp
from jax import lax
from jax.experimental import pallas as pl
from jax.experimental.pallas import tpu as pltpu
from jax.sharding import Mesh
from jax.sharding import PartitionSpec as P

D = 2048
HEADS = 64
HEAD_DIM = 64
STATE = 128
KW = 4
STEP = 4
INNER = 4096
CONV = 4352
MIX = 2 * STATE
SMALL = 384
CHUNK = 128
EDGE = 16

EPS = 1e-05
BETA_ONE = 0.5
BETA_TWO = 0.7
ADAM_EPS = 1e-08
DECAY = 0.1
rate_input = 0.02
rate_output = 0.015
rate_conv = 0.3
rate_vector = 0.5
rate_head = 0.5
HIGH = lax.Precision.HIGHEST
f32 = jnp.float32
bf16 = jnp.bfloat16
Q = ("y", "head")
ALL = ("z", "y", "head")
VMEM_LIMIT = 48 * 1024 * 1024


def dot(a, b, on_a=1, on_b=0):
    return lax.dot_general(
        a.astype(bf16), b.astype(bf16), (((on_a,), (on_b,)), ((), ())), preferred_element_type=f32
    )


def dot_exact(a, b, on_a=1, on_b=0):
    return lax.dot_general(
        a, b, (((on_a,), (on_b,)), ((), ())), preferred_element_type=f32, precision=HIGH
    )


def sigmoid(v):
    return 1.0 / (1.0 + jnp.exp(-v))


def softplus(v):
    return jnp.maximum(v, 0.0) + jnp.log1p(jnp.exp(-jnp.abs(v)))


def places(first, count, axis):
    shape = (count, 1) if axis == 0 else (1, count)
    return first + lax.broadcasted_iota(jnp.int32, shape, axis)


def segment(offsets, group, spots, sequences):
    total = jnp.zeros_like(spots)
    for k in range(sequences):
        total = total + (spots >= offsets[group, k]).astype(jnp.int32)
    return total


def lagged(current, before, own_seg, lag_segs):
    whole = jnp.concatenate([before, current], axis=0)
    rows = current.shape[0]
    edge = before.shape[0]
    out = []
    for lag in range(1, KW):
        keep = (own_seg == lag_segs[lag - 1]).astype(f32)
        out.append(whole[edge - lag : edge - lag + rows] * keep)
    return out


def conv(current, lags, taps):
    total = taps[4:5] + taps[3:4] * current
    for lag in range(1, KW):
        total = total + taps[3 - lag : 4 - lag] * lags[lag - 1]
    return total


class Place:
    def __init__(self, offsets, group, chunk, sequences):
        first = chunk * CHUNK
        at = places(first, CHUNK, 0)
        seg = functools.partial(segment, offsets, group, sequences=sequences)
        self.col = seg(at)
        self.row = seg(places(first, CHUNK, 1))
        self.lags = [seg(at - lag) for lag in range(1, KW)]
        self.ahead = [seg(at + lag) for lag in range(1, KW)]
        self.before = seg(places(first - 1, 1, 0))
        self.last = seg(places(first + CHUNK - 1, 1, 0))
        self.fresh = (self.col == self.before).astype(f32)
        self.open_end = (self.col == self.last).astype(f32)
        self.unbroken = (self.last == self.before).astype(f32)


def rows_of(ref):
    block = ref[...]
    return block.reshape(CHUNK, block.shape[-1])


def steps_of(small, pick, hp):
    raw = dot(small[:, MIX:], pick)
    shifted = raw + hp[0:1]
    step = softplus(shifted)
    log_a = -jnp.exp(hp[1:2]) * step
    lower = (
        lax.broadcasted_iota(jnp.int32, (CHUNK, CHUNK), 0)
        >= lax.broadcasted_iota(jnp.int32, (CHUNK, CHUNK), 1)
    ).astype(f32)
    running = dot_exact(lower, log_a)
    return shifted, step, log_a, running, lower


def state_kernel(sequences, offs, x, xp, xh, s, sp, sh, tx, ts, hp, pick, spread, out, carry, fall):
    group, chunk = pl.program_id(0), pl.program_id(1)
    place = Place(offs, group, chunk, sequences)

    @pl.when(chunk == 0)
    def _():
        carry[...] = jnp.zeros_like(carry)
        fall[...] = jnp.ones_like(fall)

    small = rows_of(s)
    xs = rows_of(x).astype(f32)
    prev = jnp.where(chunk == 0, xh[0], xp[0, 0]).astype(f32)
    act = conv(xs, lagged(xs, prev, place.col, place.lags), tx[...])
    values = act * sigmoid(act)
    bs = small[:, :STATE].astype(f32)
    prev_b = jnp.where(chunk == 0, sh[0], sp[0, 0])[:, :STATE].astype(f32)
    act_b = conv(bs, lagged(bs, prev_b, place.col, place.lags), ts[:, :STATE])
    keys = act_b * sigmoid(act_b)
    _, step, _, running, _ = steps_of(small, pick[...], hp[...])
    end = running[CHUNK - 1 : CHUNK]
    weight = jnp.exp(end - running) * place.open_end * step
    carried = dot_exact(jnp.broadcast_to(jnp.exp(end) * place.unbroken, (8, 128)), spread[...])[0:1]
    memory = carried * carry[...] + dot(keys, values * dot_exact(weight, spread[...]), 0, 0)
    total = fall[0:1] * carried
    carry[...] = memory
    fall[...] = jnp.broadcast_to(total, fall.shape)

    @pl.when(chunk == pl.num_programs(1) - 1)
    def _():
        high = total.astype(bf16)
        middle = (total - high.astype(f32)).astype(bf16)
        low = (total - high.astype(f32) - middle.astype(f32)).astype(bf16)
        out[0, :STATE] = memory.astype(bf16)
        out[0, STATE:] = jnp.concatenate(
            [high, middle, low, jnp.zeros((EDGE - 3, high.shape[1]), bf16)], axis=0
        )


def scan_kernel(sequences, offs, x, xp, xh, s, sp, sh, tx, ts, hp, pick, spread, first, out, kept, carry):
    group, chunk = pl.program_id(0), pl.program_id(1)
    place = Place(offs, group, chunk, sequences)

    @pl.when(chunk == 0)
    def _():
        carry[...] = first[0]

    memory = carry[...]
    kept[0, 0] = memory
    small = rows_of(s)
    xs = rows_of(x).astype(f32)
    prev = jnp.where(chunk == 0, xh[0], xp[0, 0]).astype(f32)
    act = conv(xs, lagged(xs, prev, place.col, place.lags), tx[...])
    values = act * sigmoid(act)
    mix = small[:, :MIX].astype(f32)
    prev_m = jnp.where(chunk == 0, sh[0], sp[0, 0])[:, :MIX].astype(f32)
    act_m = conv(mix, lagged(mix, prev_m, place.col, place.lags), ts[...])
    act_m = act_m * sigmoid(act_m)
    keys, queries = act_m[:, :STATE], act_m[:, STATE:]
    _, step, _, running, lower = steps_of(small, pick[...], hp[...])
    end = running[CHUNK - 1 : CHUNK]
    inflow = jnp.exp(running) * place.fresh
    weight = jnp.exp(end - running) * place.open_end
    carried = jnp.exp(end) * place.unbroken
    wide = dot_exact(
        jnp.concatenate([step, inflow, weight, jnp.broadcast_to(carried, (8, 128)), hp[...]], axis=0),
        spread[...],
    )
    step_w, inflow_w, weight_w = (wide[i * CHUNK : (i + 1) * CHUNK] for i in range(3))
    carried_w = wide[3 * CHUNK : 3 * CHUNK + 1]
    skip_w = wide[3 * CHUNK + 10 : 3 * CHUNK + 11]
    weighted = values * step_w
    within = (place.col == place.row) & (lower > 0.5)
    scores = dot(queries, keys, 1, 1)
    running_t = running.T
    left = lax.broadcasted_iota(jnp.int32, (1, 128), 1) < HEAD_DIM
    from_memory = dot(queries, memory) * inflow_w + skip_w * values
    for pair in range(values.shape[1] // 128):
        lanes = slice(128 * pair, 128 * pair + 128)
        mixed = []
        for h in (2 * pair, 2 * pair + 1):
            gaps = running[:, h : h + 1] - running_t[h : h + 1, :]
            mixed.append(scores * jnp.exp(jnp.where(within, gaps, -1e30)))
        part = weighted[:, lanes]
        both = jnp.concatenate([jnp.where(left, part, 0.0), jnp.where(left, 0.0, part)], axis=0)
        result = dot(jnp.concatenate(mixed, axis=1), both) + from_memory[:, lanes]
        out[:, 0, :, lanes] = result.astype(bf16).reshape(out.shape[0], out.shape[2], 128)
    carry[...] = carried_w * memory + dot(keys, weighted * weight_w, 0, 0)


def direct_kernel(sequences, offs, s, sp, sh, ts, hp, pick, spread, dy, out, carry, fall):
    group, chunk = pl.program_id(0), pl.program_id(1)
    place = Place(offs, group, chunk, sequences)

    @pl.when(chunk == 0)
    def _():
        carry[...] = jnp.zeros_like(carry)
        fall[...] = jnp.ones_like(fall)

    small = rows_of(s)
    cs = small[:, STATE:MIX].astype(f32)
    prev_c = jnp.where(chunk == 0, sh[0], sp[0, 0])[:, STATE:MIX].astype(f32)
    act_c = conv(cs, lagged(cs, prev_c, place.col, place.lags), ts[:, STATE:])
    queries = act_c * sigmoid(act_c)
    _, _, _, running, _ = steps_of(small, pick[...], hp[...])
    end = running[CHUNK - 1 : CHUNK]
    wide = dot_exact(
        jnp.concatenate(
            [
                jnp.exp(running) * place.fresh,
                jnp.broadcast_to(jnp.exp(end) * place.unbroken, (8, 128)),
            ],
            axis=0,
        ),
        spread[...],
    )
    grad = rows_of(dy).astype(f32) * wide[:CHUNK]
    total = carry[...] + fall[0:1] * dot(queries, grad, 0, 0)
    carry[...] = total
    fall[...] = fall[...] * wide[CHUNK : CHUNK + 1]

    @pl.when(chunk == pl.num_programs(1) - 1)
    def _():
        out[0] = total.astype(bf16)


def conv_back(du, ahead, taps, own_seg, ahead_segs):
    rows = du.shape[0]
    whole = jnp.concatenate([du, ahead], axis=0)
    total = taps[3:4] * du
    for lag in range(1, KW):
        keep = (own_seg == ahead_segs[lag - 1]).astype(f32)
        total = total + taps[3 - lag : 4 - lag] * (whole[lag : lag + rows] * keep)
    return total


def conv_rim(du, taps, seg):
    at = places(-EDGE, EDGE, 0)
    whole = jnp.concatenate([jnp.zeros((EDGE, du.shape[1]), f32), du[:EDGE]], axis=0)
    total = jnp.zeros((EDGE, du.shape[1]), f32)
    for lag in range(1, KW):
        keep = (seg(at) == seg(at + lag)).astype(f32)
        total = total + taps[3 - lag : 4 - lag] * (whole[lag : lag + EDGE] * keep)
    return total


def column_sums(du, current, lags):
    rows = [jnp.sum(du * lags[KW - 2 - k], axis=0, keepdims=True) for k in range(KW - 1)]
    rows.append(jnp.sum(du * current, axis=0, keepdims=True))
    rows.append(jnp.sum(du, axis=0, keepdims=True))
    return rows


def back_kernel(
    sequences, offs, x, xp, xh, s, sp, sh, tx, ts, hp, pick, spread, dy, kept, later,
    dx, ds, tail_x, tail_s, rim_x, rim_s, gx, gs, gh, carry, next_x, next_s,
):
    group = pl.program_id(0)
    chunks = pl.num_programs(1)
    chunk = chunks - 1 - pl.program_id(1)
    place = Place(offs, group, chunk, sequences)
    seg = functools.partial(segment, offs, group, sequences=sequences)
    width = tx.shape[1]
    head_count = width // HEAD_DIM

    @pl.when(pl.program_id(1) == 0)
    def _():
        carry[...] = later[0]
        next_x[...] = jnp.zeros_like(next_x)
        next_s[...] = jnp.zeros_like(next_s)

    @pl.when((pl.program_id(1) == 0) & (group == 0))
    def _():
        gx[...] = jnp.zeros_like(gx)
        gs[...] = jnp.zeros_like(gs)
        gh[...] = jnp.zeros_like(gh)

    small = rows_of(s)
    xs = rows_of(x).astype(f32)
    prev = jnp.where(chunk == 0, xh[0], xp[0, 0]).astype(f32)
    lags_x = lagged(xs, prev, place.col, place.lags)
    act = conv(xs, lags_x, tx[...])
    gate = sigmoid(act)
    values = act * gate
    slope_x = gate * (1.0 + act * (1.0 - gate))
    mix = small[:, :MIX].astype(f32)
    prev_m = jnp.where(chunk == 0, sh[0], sp[0, 0])[:, :MIX].astype(f32)
    lags_m = lagged(mix, prev_m, place.col, place.lags)
    act_m = conv(mix, lags_m, ts[...])
    gate_m = sigmoid(act_m)
    keys, queries = (act_m * gate_m)[:, :STATE], (act_m * gate_m)[:, STATE:]
    slope_m = gate_m * (1.0 + act_m * (1.0 - gate_m))
    shifted, step, log_a, running, lower = steps_of(small, pick[...], hp[...])
    end = running[CHUNK - 1 : CHUNK]
    carried = jnp.exp(end) * place.unbroken
    wide = dot_exact(
        jnp.concatenate(
            [
                step,
                jnp.exp(running) * place.fresh,
                jnp.exp(end - running) * place.open_end,
                jnp.broadcast_to(carried, (8, 128)),
                hp[...],
            ],
            axis=0,
        ),
        spread[...],
    )
    step_w, inflow_w, weight_w = (wide[i * CHUNK : (i + 1) * CHUNK] for i in range(3))
    carried_w = wide[3 * CHUNK : 3 * CHUNK + 1]
    skip_w = wide[3 * CHUNK + 10 : 3 * CHUNK + 11]
    grad = rows_of(dy).astype(f32)
    weighted = values * step_w
    memory = kept[0, 0]
    back = carry[...]

    scores = dot(queries, keys, 1, 1)
    running_t = running.T
    within = (place.col == place.row) & (lower > 0.5)
    left = lax.broadcasted_iota(jnp.int32, (1, 128), 1) < HEAD_DIM
    lane = lax.broadcasted_iota(jnp.int32, (1, 128), 1)

    grad_in = grad * inflow_w
    to_end = weighted * weight_w
    back_values = dot(keys, back) * weight_w
    from_state = weighted * back_values
    grad_run = grad_in * dot(queries, memory) - from_state
    grad_scores = jnp.zeros((CHUNK, CHUNK), f32)
    run_cols = jnp.zeros((CHUNK, 128), f32)
    run_rows = []
    back_weighted = []
    for pair in range(width // 128):
        lanes = slice(128 * pair, 128 * pair + 128)
        decays = []
        for h in (2 * pair, 2 * pair + 1):
            gaps = running[:, h : h + 1] - running_t[h : h + 1, :]
            decays.append(jnp.exp(jnp.where(within, gaps, -1e30)))
        decay = jnp.concatenate(decays, axis=0)
        mixed = jnp.concatenate([scores, scores], axis=0) * decay
        part = grad[:, lanes]
        both = jnp.concatenate([jnp.where(left, part, 0.0), jnp.where(left, 0.0, part)], axis=0)
        grad_mixed = dot(both, weighted[:, lanes], 1, 1)
        through = grad_mixed * decay
        grad_scores = grad_scores + through[:CHUNK] + through[CHUNK:]
        pull = grad_mixed * mixed
        sums = jnp.sum(pull, axis=1, keepdims=True)
        run_cols = run_cols + jnp.where(lane == 2 * pair, sums[:CHUNK], 0.0)
        run_cols = run_cols + jnp.where(lane == 2 * pair + 1, sums[CHUNK:], 0.0)
        run_rows.append(jnp.sum(pull[:CHUNK], axis=0, keepdims=True))
        run_rows.append(jnp.sum(pull[CHUNK:], axis=0, keepdims=True))
        back_weighted.append(dot(mixed, both, 0, 0) + back_values[:, lanes])
    back_weighted = jnp.concatenate(back_weighted, axis=1)
    run_rows.append(jnp.zeros((CHUNK - head_count, CHUNK), f32))
    run_cols = run_cols - jnp.concatenate(run_rows, axis=0).T

    grad_queries = dot(grad_scores, keys) + dot(grad_in, memory, 1, 1)
    grad_keys = dot(grad_scores, queries, 0, 0) + dot(to_end, back, 1, 1)
    end_sum = jnp.sum(from_state, axis=0, keepdims=True) + carried_w * jnp.sum(
        back * memory, axis=0, keepdims=True
    )
    carry[...] = carried_w * back + dot(queries, grad_in, 0, 0)

    narrow = dot_exact(
        jnp.concatenate(
            [grad_run, back_weighted * values, jnp.broadcast_to(end_sum, (8, width))], axis=0
        ),
        spread[...],
        1,
        1,
    )
    grad_log = dot_exact(lower, run_cols + narrow[:CHUNK], 0, 0) + narrow[2 * CHUNK : 2 * CHUNK + 1]
    rate = -jnp.exp(hp[1:2])
    grad_step = (narrow[CHUNK : 2 * CHUNK] + grad_log * rate) * sigmoid(shifted)
    gh[0:1] += jnp.sum(grad_step, axis=0, keepdims=True)
    gh[1:2] += jnp.sum(grad_log * log_a, axis=0, keepdims=True)

    du_x = (back_weighted * step_w + skip_w * grad) * slope_x
    du_m = jnp.concatenate([grad_keys, grad_queries], axis=1) * slope_m
    rows = column_sums(du_x, xs, lags_x)
    rows.append(jnp.sum(grad * values, axis=0, keepdims=True))
    rows.append(jnp.zeros((2, width), f32))
    gx[...] += jnp.concatenate(rows, axis=0)
    rows = column_sums(du_m, mix, lags_m)
    rows.append(jnp.zeros((3, MIX), f32))
    gs[...] += jnp.concatenate(rows, axis=0)

    grad_x = conv_back(du_x, next_x[...], tx[...], place.col, place.ahead)
    grad_m = conv_back(du_m, next_s[...], ts[...], place.col, place.ahead)
    next_x[...] = du_x[:8]
    next_s[...] = du_m[:8]
    shape = (dx.shape[0], dx.shape[2])
    dx[:, 0] = grad_x.astype(bf16).reshape(shape + (width,))
    ds[:, 0, :, :MIX] = grad_m.astype(bf16).reshape(shape + (MIX,))
    placed = dot(grad_step, pick[...], 1, 1)
    ds[:, 0, :, MIX:] = placed.astype(bf16).reshape(shape + (SMALL - MIX,))

    @pl.when(chunk == chunks - 1)
    def _():
        tail_x[0] = grad_x[CHUNK - EDGE :]
        tail_s[0] = grad_m[CHUNK - EDGE :]

    @pl.when(chunk == 0)
    def _():
        rim_x[0] = conv_rim(du_x, tx[...], seg)
        rim_s[0] = conv_rim(du_m, ts[...], seg)


def adam(weight, first, second, grad, rate):
    first_new = BETA_ONE * first + (1.0 - BETA_ONE) * grad
    second_new = BETA_TWO * second + (1.0 - BETA_TWO) * grad * grad
    update = (
        first_new
        / (1.0 - BETA_ONE**STEP)
        / (jnp.sqrt(second_new / (1.0 - BETA_TWO**STEP)) + ADAM_EPS)
    )
    return (weight - rate * (update + DECAY * weight), first_new, second_new)


def shifted_along(value, axis, by):
    peers = lax.axis_size(axis)
    pairs = [(i, i + by) for i in range(peers) if 0 <= i + by < peers]
    return lax.ppermute(value, axis, pairs)


def three_parts(value):
    high = lax.reduce_precision(value, 8, 7)
    middle = lax.reduce_precision(value - high, 8, 7)
    low = value - high - middle
    return jnp.stack([high, middle, low]).astype(bf16)


def product(a, b, on_a, on_b):
    return lax.dot_general(a, b, (((on_a,), (on_b,)), ((), ())), preferred_element_type=f32)


def local(
    x_in, lengths, cotangent, w_in, m_in, v_in, w_out, m_out, v_out, conv_w, m_conv, v_conv,
    vectors, m_vec, v_vec, head_params, m_head, v_head,
):
    zn = lax.axis_size("z")
    head_size = lax.axis_size("head")
    qn = lax.axis_size("y") * head_size
    devices = zn * qn
    q = lax.axis_index(Q)
    z = lax.axis_index("z")
    groups, own, _ = x_in.shape
    span = own * qn
    sequences = lengths.shape[1]
    chunks = span // CHUNK
    part = CHUNK // own
    tokens = groups * span
    width = INNER // qn
    heads_own = HEADS // qn
    unit = INNER // devices
    strided = unit % HEAD_DIM == 0
    rows_in = D // devices
    conv_rows, vec_rows, head_cols = conv_w.shape[0], vectors.shape[0], head_params.shape[1]

    def split(array, size):
        lead = array.shape[:-1]
        if strided:
            array = array.reshape(lead + (zn, qn, size // devices))
        else:
            array = array.reshape(lead + (1, qn, size // qn))
        return jnp.moveaxis(array, -2, 0).reshape((qn,) + lead + (size // qn,))

    def join(array, size):
        lead = array.shape[1:-1]
        count = zn if strided else 1
        array = array.reshape((qn,) + lead + (count, size // (qn * count)))
        return jnp.moveaxis(array, 0, -2).reshape(lead + (size,))

    def own_of(array, size):
        return lax.dynamic_index_in_dim(split(array, size), q, 0, False)

    own_heads = own_of(jnp.arange(HEADS, dtype=jnp.int32), HEADS)

    payload = jnp.concatenate(
        [
            conv_w.astype(bf16).T.reshape(-1),
            vectors.astype(bf16),
            three_parts(head_params).reshape(-1),
        ]
    )
    payload = jnp.pad(payload, (0, rows_in * HEADS - payload.shape[0])).reshape(rows_in, HEADS)
    small_own = jnp.concatenate([w_in[:, 2 * INNER :].astype(bf16), payload], axis=1)
    small_all = lax.all_gather(small_own, ALL, axis=0, tiled=False)
    w_small = small_all.reshape(D, SMALL)
    payload = small_all[:, :, SMALL - HEADS :].reshape(devices, rows_in * HEADS)
    cut = [conv_rows * KW, vec_rows, 9 * head_cols]
    taps = jnp.moveaxis(payload[:, : cut[0]].reshape(devices, KW, conv_rows), 0, 1)
    taps = taps.reshape(KW, CONV).astype(f32)
    vec = payload[:, cut[0] : cut[0] + cut[1]].reshape(-1).astype(f32)
    params = payload[:head_size, cut[0] + cut[1] : sum(cut)].astype(f32)
    params = jnp.sum(params.reshape(head_size, 3, 3, head_cols), axis=1)
    params = jnp.moveaxis(params, 0, 1).reshape(3, HEADS)
    norm_gain = vec[:D]
    conv_bias = vec[D : D + CONV]
    gate_gain = own_of(vec[D + CONV :], INNER)
    table = jnp.concatenate([taps, conv_bias[None], jnp.zeros((3, CONV), f32)], axis=0)
    taps_x = own_of(table[:, :INNER], INNER)
    taps_s = table[:, INNER:]
    lanes = jnp.arange(128, dtype=jnp.int32)
    head_of_lane = jnp.pad(own_heads, (0, 128 - heads_own), constant_values=-1)
    pick = (lanes[:, None] == head_of_lane[None, :]).astype(bf16)
    hp = jnp.sum(
        jnp.where(jnp.arange(HEADS)[:, None] == head_of_lane[None, :], params[:, :, None], 0.0), 1
    )
    hp = jnp.pad(hp, ((0, 5), (0, 0)))
    spread = (lanes[:, None] == jnp.arange(width)[None, :] // HEAD_DIM).astype(f32)
    offsets = (jnp.cumsum(lengths, axis=1) - lengths - z * span).astype(jnp.int32)

    x_all = lax.all_gather(x_in, Q, axis=0, tiled=False).reshape(tokens, D)
    cot_all = lax.all_gather(cotangent, Q, axis=0, tiled=False).reshape(tokens, D)

    def columns(first):
        mine = split(w_in[:, first : first + INNER].astype(bf16), INNER)
        mine = lax.all_to_all(mine, Q, split_axis=0, concat_axis=0, tiled=True)
        return lax.all_gather(mine, "z", axis=0, tiled=False).reshape(D, width)

    w_x = columns(INNER)
    w_z = columns(0)
    if strided:
        w_o = lax.all_gather(w_out.astype(bf16), "z", axis=0, tiled=True)
    else:
        w_o = lax.all_gather(w_out.astype(bf16), ALL, axis=0, tiled=True)
        w_o = lax.dynamic_slice_in_dim(w_o, q * width, width, 0)

    x_float = x_all.astype(f32)
    x_scaled = x_float * lax.rsqrt(jnp.mean(x_float * x_float, axis=-1, keepdims=True) + EPS)
    normed = (x_scaled * norm_gain).astype(bf16)
    token_shape = (qn, groups, own)
    x_raw = product(normed, w_x, 1, 0).astype(bf16).reshape(token_shape + (width,))
    s_raw = product(normed, w_small, 1, 0).astype(bf16).reshape(token_shape + (SMALL,))
    x_halo = shifted_along(x_raw[qn - 1, :, own - EDGE :], "z", 1)
    s_halo = shifted_along(s_raw[qn - 1, :, own - EDGE :], "z", 1)

    def at(reverse):
        return (lambda i: chunks - 1 - i) if reverse else (lambda i: i)

    def token_spec(cols, reverse):
        return pl.BlockSpec((part, 1, own, cols), lambda g, i: (at(reverse)(i), g, 0, 0))

    def before_spec(cols, reverse):
        return pl.BlockSpec(
            (1, 1, EDGE, cols),
            lambda g, i: (jnp.maximum(part * at(reverse)(i) - 1, 0), g, own // EDGE - 1, 0),
        )

    def group_spec(*dims):
        return pl.BlockSpec((1,) + dims, lambda g, i: (g,) + (0,) * len(dims))

    def whole_spec(*dims):
        return pl.BlockSpec(dims, lambda g, i: (0,) * len(dims))

    def kept_spec(reverse):
        return pl.BlockSpec((1, 1, STATE, width), lambda g, i: (g, at(reverse)(i), 0, 0))

    offs_spec = pl.BlockSpec(memory_space=pltpu.SMEM)

    def x_specs(reverse):
        return [token_spec(width, reverse), before_spec(width, reverse), group_spec(EDGE, width)]

    def s_specs(reverse):
        return [token_spec(SMALL, reverse), before_spec(SMALL, reverse), group_spec(EDGE, SMALL)]

    head_specs = [whole_spec(8, 128), whole_spec(128, 128), whole_spec(128, width)]
    x_args = (x_raw, x_raw, x_halo)
    s_args = (s_raw, s_raw, s_halo)
    head_args = (hp, pick, spread)
    state_ref = pltpu.VMEM((STATE, width), f32)
    fall_ref = pltpu.VMEM((8, width), f32)

    def call(kernel, in_specs, out_specs, out_shape, scratch, flops, moved):
        return pl.pallas_call(
            functools.partial(kernel, sequences),
            grid=(groups, chunks),
            in_specs=in_specs,
            out_specs=out_specs,
            out_shape=out_shape,
            scratch_shapes=scratch,
            compiler_params=pltpu.CompilerParams(
                dimension_semantics=("arbitrary", "arbitrary"), vmem_limit_bytes=VMEM_LIMIT
            ),
            cost_estimate=pl.CostEstimate(flops=flops, bytes_accessed=moved, transcendentals=0),
        )

    with jax.named_scope("memory_own"):
        ended = call(
            state_kernel,
            [offs_spec] + x_specs(False) + s_specs(False)
            + [whole_spec(8, width), whole_spec(8, MIX)] + head_specs,
            group_spec(STATE + EDGE, width),
            jax.ShapeDtypeStruct((groups, STATE + EDGE, width), bf16),
            [state_ref, fall_ref],
            4_000_000_000, 4_000_000,
        )(offsets, *x_args, *s_args, taps_x, taps_s, *head_args)
    ended_all = lax.all_gather(ended, "z", axis=0, tiled=False).astype(f32)
    falls = jnp.sum(ended_all[:, :, STATE : STATE + 3], axis=2, keepdims=True)
    incoming = jnp.zeros((groups, STATE, width), f32)
    for k in range(zn - 1):
        joined = falls[k] * incoming + ended_all[k, :, :STATE]
        incoming = jnp.where(k < z, joined, incoming)

    with jax.named_scope("scan"):
        scanned, kept = call(
            scan_kernel,
            [offs_spec] + x_specs(False) + s_specs(False)
            + [whole_spec(8, width), whole_spec(8, MIX)] + head_specs + [group_spec(STATE, width)],
            [token_spec(width, False), kept_spec(False)],
            [
                jax.ShapeDtypeStruct(token_shape + (width,), bf16),
                jax.ShapeDtypeStruct((groups, chunks, STATE, width), f32),
            ],
            [state_ref],
            8_000_000_000, 6_000_000,
        )(offsets, *x_args, *s_args, taps_x, taps_s, *head_args, incoming)

    gate_in = product(normed, w_z, 1, 0)
    grad_gnorm = product(cot_all, w_o, 1, 1)
    scan_b = scanned.reshape(tokens, width).astype(f32)
    gate_sig = jax.nn.sigmoid(gate_in)
    gate = gate_in * gate_sig
    gated = scan_b * gate
    grad_gain_in = grad_gnorm * gate_gain
    sums = jnp.stack([jnp.sum(gated * gated, axis=1), jnp.sum(grad_gain_in * gated, axis=1)])
    sums = lax.psum(sums, Q) / INNER
    inverse = lax.rsqrt(sums[0] + EPS)[:, None]
    gated_unit = gated * inverse
    gnorm = (gated_unit * gate_gain).astype(bf16)
    grad_gate_gain = jnp.sum(grad_gnorm * gated_unit, axis=0)
    grad_gated = inverse * (grad_gain_in - gated * (inverse * inverse * sums[1][:, None]))
    grad_scan = (grad_gated * gate).astype(bf16).reshape(token_shape + (width,))
    slope = gate_sig * (1.0 + gate_in * (1.0 - gate_sig))
    grad_z = (grad_gated * scan_b * slope).astype(bf16)

    branch = product(gnorm, w_o, 1, 0).astype(bf16).reshape(qn, groups, own, D)
    branch = lax.psum_scatter(branch, Q, scatter_dimension=0, tiled=False)
    result = (x_in.astype(f32) + branch.astype(f32)).astype(bf16)
    grad_out = product(gnorm, cot_all, 0, 0).astype(bf16)
    if strided:
        grad_out = lax.psum_scatter(grad_out, "z", scatter_dimension=0, tiled=True)
    else:
        full = jnp.zeros((INNER, D), bf16)
        full = lax.dynamic_update_slice_in_dim(full, grad_out, q * width, 0)
        grad_out = lax.psum_scatter(full, ALL, scatter_dimension=0, tiled=True)

    with jax.named_scope("memory_back"):
        direct = call(
            direct_kernel,
            [offs_spec] + s_specs(False) + [whole_spec(8, MIX)] + head_specs
            + [token_spec(width, False)],
            group_spec(STATE, width),
            jax.ShapeDtypeStruct((groups, STATE, width), bf16),
            [state_ref, fall_ref],
            2_000_000_000, 3_000_000,
        )(offsets, *s_args, taps_s, *head_args, grad_scan)
    direct_all = lax.all_gather(direct, "z", axis=0, tiled=False).astype(f32)
    later = jnp.zeros((groups, STATE, width), f32)
    for k in range(zn - 1, 0, -1):
        joined = falls[k] * later + direct_all[k]
        later = jnp.where(k > z, joined, later)

    def home(grad):
        cols = grad.shape[1]
        grad = grad.astype(bf16).reshape(zn, qn, rows_in, cols)
        grad = lax.psum_scatter(grad, "z", scatter_dimension=0, tiled=False)
        return lax.all_to_all(grad, Q, split_axis=0, concat_axis=0, tiled=True)

    home_z = home(product(normed, grad_z, 0, 0))

    with jax.named_scope("scan_back"):
        dx, ds, tail_x, tail_s, rim_x, rim_s, gx, gs, gh = call(
            back_kernel,
            [offs_spec] + x_specs(True) + s_specs(True)
            + [whole_spec(8, width), whole_spec(8, MIX)] + head_specs
            + [token_spec(width, True), kept_spec(True), group_spec(STATE, width)],
            [
                token_spec(width, True), token_spec(SMALL, True),
                group_spec(EDGE, width), group_spec(EDGE, MIX),
                group_spec(EDGE, width), group_spec(EDGE, MIX),
                whole_spec(8, width), whole_spec(8, MIX), whole_spec(8, 128),
            ],
            [
                jax.ShapeDtypeStruct(token_shape + (width,), bf16),
                jax.ShapeDtypeStruct(token_shape + (SMALL,), bf16),
                jax.ShapeDtypeStruct((groups, EDGE, width), f32),
                jax.ShapeDtypeStruct((groups, EDGE, MIX), f32),
                jax.ShapeDtypeStruct((groups, EDGE, width), f32),
                jax.ShapeDtypeStruct((groups, EDGE, MIX), f32),
                jax.ShapeDtypeStruct((8, width), f32),
                jax.ShapeDtypeStruct((8, MIX), f32),
                jax.ShapeDtypeStruct((8, 128), f32),
            ],
            [state_ref, pltpu.VMEM((8, width), f32), pltpu.VMEM((8, MIX), f32)],
            16_000_000_000, 9_000_000,
        )(offsets, *x_args, *s_args, taps_x, taps_s, *head_args, grad_scan, kept, later)
    rim_x, rim_s = shifted_along(rim_x, "z", -1), shifted_along(rim_s, "z", -1)
    dx = dx.at[qn - 1, :, own - EDGE :].set((tail_x + rim_x).astype(bf16))
    ds = ds.at[qn - 1, :, own - EDGE :, :MIX].set((tail_s + rim_s).astype(bf16))
    grad_x = dx.reshape(tokens, width)
    grad_s = ds.reshape(tokens, SMALL)

    home_x = home(product(normed, grad_x, 0, 0))
    home_s = home(product(normed, grad_s, 0, 0))
    grad_in = jnp.concatenate(
        [
            join(home_z, INNER),
            join(home_x, INNER),
            jnp.sum(home_s.astype(f32), axis=0)[:, : MIX + HEADS].astype(bf16),
        ],
        axis=1,
    ).astype(f32)

    grad_normed = (
        product(grad_z, w_z, 1, 1) + product(grad_x, w_x, 1, 1) + product(grad_s, w_small, 1, 1)
    )
    grad_norm_gain = jnp.sum(grad_normed * x_scaled, axis=0)
    grad_own = lax.psum_scatter(
        grad_normed.astype(bf16).reshape(qn, groups, own, D), Q, scatter_dimension=0, tiled=False
    ).astype(f32)
    x_own = x_in.astype(f32)
    inverse = lax.rsqrt(jnp.mean(x_own * x_own, axis=-1, keepdims=True) + EPS)
    grad_unit = grad_own * norm_gain
    pulled = jnp.mean(grad_unit * x_own, axis=-1, keepdims=True)
    grad_x_own = inverse * (grad_unit - x_own * (inverse * inverse * pulled))
    input_grad = (grad_x_own + cotangent.astype(f32)).astype(bf16)

    def place_own(array, size):
        mine = (jnp.arange(qn) == q).astype(f32).reshape((qn,) + (1,) * array.ndim)
        return join(array[None] * mine, size)

    table = jnp.concatenate([place_own(gx[:5], INNER), gs[:5]], axis=1)
    grad_vec = jnp.concatenate([grad_norm_gain, table[4], place_own(grad_gate_gain, INNER)])
    grad_skip = jnp.sum(gx[5].reshape(heads_own, HEAD_DIM), axis=1)
    grad_heads = jnp.concatenate([gh[:2, :heads_own], grad_skip[None]], axis=0)
    grad_heads = place_own(grad_heads, HEADS).reshape(3, head_size, head_cols)
    grad_heads = jnp.moveaxis(grad_heads, 1, 0).reshape(1, head_size, 3 * head_cols)
    grad_heads = jnp.broadcast_to(grad_heads, (devices // head_size,) + grad_heads.shape[1:])
    packed = jnp.concatenate(
        [
            jnp.moveaxis(table[:4].reshape(KW, devices, conv_rows), 1, 0).reshape(devices, -1),
            grad_vec.reshape(devices, vec_rows),
            grad_heads.reshape(devices, -1),
        ],
        axis=1,
    )
    used = packed.shape[1]
    packed = jnp.pad(packed, ((0, 0), (0, -used % 1024))).reshape(devices, -1, 128)
    packed = lax.psum_scatter(packed, ALL, scatter_dimension=0, tiled=False).reshape(-1)
    grad_conv = packed[: conv_rows * KW].reshape(KW, conv_rows).T
    grad_vec = packed[conv_rows * KW : conv_rows * KW + vec_rows]
    grad_head = packed[conv_rows * KW + vec_rows : used].reshape(3, head_cols)

    in_new = adam(w_in, m_in, v_in, grad_in, rate_input)
    out_new = adam(w_out, m_out, v_out, grad_out.astype(f32), rate_output)
    conv_new = adam(conv_w, m_conv, v_conv, grad_conv, rate_conv)
    vec_new = adam(vectors, m_vec, v_vec, grad_vec, rate_vector)
    head_new = adam(head_params, m_head, v_head, grad_head, rate_head)
    return (result, input_grad, *in_new, *out_new, *conv_new, *vec_new, *head_new)


def solution(mesh):
    seq, head = mesh.shape["seq"], mesh.shape["head"]
    fine = Mesh(mesh.devices.reshape(seq // 2, 2, head), ALL)
    token, row = P(None, ALL, None), P(ALL, None)
    line, heads = P(ALL), P(None, "head")
    return jax.shard_map(
        local,
        mesh=fine,
        in_specs=(token, P(), token) + (row,) * 9 + (line,) * 3 + (heads,) * 3,
        out_specs=(token, token) + (row,) * 9 + (line,) * 3 + (heads,) * 3,
        check_vma=False,
    )
```

```python
import functools

import jax
import jax.numpy as jnp
from jax import lax
from jax.experimental import pallas as pl
from jax.experimental.pallas import tpu as pltpu
from jax.sharding import Mesh
from jax.sharding import PartitionSpec as P

D = 2048
HEADS = 64
HEAD_DIM = 64
STATE = 128
KW = 4
STEP = 4
INNER = 4096
CONV = 4352
MIX = 2 * STATE
SMALL = 384
CHUNK = 128
EDGE = 16

EPS = 1e-05
BETA_ONE = 0.5
BETA_TWO = 0.7
ADAM_EPS = 1e-08
DECAY = 0.1
rate_input = 0.02
rate_output = 0.015
rate_conv = 0.3
rate_vector = 0.5
rate_head = 0.5
HIGH = lax.Precision.HIGHEST
f32 = jnp.float32
bf16 = jnp.bfloat16
ROW = ("zh", "y")
Q = ("zl", "x", "core")
ALL = ("zh", "zl", "y", "x", "core")
VMEM_LIMIT = 48 * 1024 * 1024


def cost(us):
    return pl.CostEstimate(flops=int(us * 0.4e9), bytes_accessed=1000, transcendentals=0)


def dot(a, b, on_a=1, on_b=0):
    return lax.dot_general(
        a.astype(bf16), b.astype(bf16), (((on_a,), (on_b,)), ((), ())), preferred_element_type=f32
    )


def split_two(value):
    high = value.astype(bf16)
    return high, (value - high.astype(f32)).astype(bf16)


def widen(value, spread):
    return dot(jnp.concatenate(split_two(value), axis=1), spread)


def narrow(value, spread):
    high, low = split_two(value)
    ones = spread[:128]
    return dot(high, ones, 1, 1) + dot(low, ones, 1, 1)


def running_sum(lower, value, on=1):
    high, middle = split_two(value)
    low = (value - high.astype(f32) - middle.astype(f32)).astype(bf16)
    parts = jnp.concatenate([high, middle, low], axis=0)
    return dot(jnp.concatenate([lower] * 3, axis=on), parts, on, 0)


def sigmoid(v):
    return 0.5 * jnp.tanh(0.5 * v) + 0.5


def softplus(v):
    return jnp.maximum(v, 0.0) + jnp.log1p(jnp.exp(-jnp.abs(v)))


def places(first, count, axis):
    shape = (count, 1) if axis == 0 else (1, count)
    return first + lax.broadcasted_iota(jnp.int32, shape, axis)


def segment(offsets, group, spots, sequences):
    total = jnp.zeros_like(spots)
    for k in range(sequences):
        total = total + (spots >= offsets[group, k]).astype(jnp.int32)
    return total


def lagged(current, before, own_seg, lag_segs):
    whole = jnp.concatenate([before, current], axis=0)
    rows = current.shape[0]
    edge = before.shape[0]
    out = []
    for lag in range(1, KW):
        keep = (own_seg == lag_segs[lag - 1]).astype(f32)
        out.append(whole[edge - lag : edge - lag + rows] * keep)
    return out


def conv(current, lags, taps):
    total = taps[4:5] + taps[3:4] * current
    for lag in range(1, KW):
        total = total + taps[3 - lag : 4 - lag] * lags[lag - 1]
    return total


class Place:
    def __init__(self, offsets, group, chunk, sequences):
        first = chunk * CHUNK
        at = places(first, CHUNK, 0)
        seg = functools.partial(segment, offsets, group, sequences=sequences)
        self.col = seg(at)
        self.row = seg(places(first, CHUNK, 1))
        self.lags = [seg(at - lag) for lag in range(1, KW)]
        self.ahead = [seg(at + lag) for lag in range(1, KW)]
        self.before = seg(places(first - 1, 1, 0))
        self.last = seg(places(first + CHUNK - 1, 1, 0))
        self.fresh = (self.col == self.before).astype(f32)
        self.open_end = (self.col == self.last).astype(f32)
        self.unbroken = (self.last == self.before).astype(f32)


def rows_of(ref):
    block = ref[...]
    return block.reshape(CHUNK, block.shape[-1])


def steps_of(small, pick, hp):
    raw = dot(small[:, MIX:], pick)
    shifted = raw + hp[0:1]
    step = softplus(shifted)
    log_a = -jnp.exp(hp[1:2]) * step
    lower = (
        lax.broadcasted_iota(jnp.int32, (CHUNK, CHUNK), 0)
        >= lax.broadcasted_iota(jnp.int32, (CHUNK, CHUNK), 1)
    ).astype(f32)
    running = running_sum(lower, log_a)
    return shifted, step, log_a, running, lower


def pack(out, memory, fall):
    high = fall.astype(bf16)
    middle = (fall - high.astype(f32)).astype(bf16)
    low = (fall - high.astype(f32) - middle.astype(f32)).astype(bf16)
    out[0, :STATE] = memory.astype(bf16)
    out[0, STATE:] = jnp.concatenate(
        [high, middle, low, jnp.zeros((EDGE - 3, high.shape[1]), bf16)], axis=0
    )


def state_kernel(sequences, offs, x, xp, xh, s, sp, sh, tx, ts, hp, pick, spread, out, carry, fall):
    group, chunk = pl.program_id(0), pl.program_id(1)
    place = Place(offs, group, chunk, sequences)

    @pl.when(chunk == 0)
    def _():
        carry[...] = jnp.zeros_like(carry)
        fall[...] = jnp.ones_like(fall)

    small = rows_of(s)
    xs = rows_of(x).astype(f32)
    prev = jnp.where(chunk == 0, xh[0], xp[0, 0]).astype(f32)
    act = conv(xs, lagged(xs, prev, place.col, place.lags), tx[...])
    values = act * sigmoid(act)
    bs = small[:, :STATE].astype(f32)
    prev_b = jnp.where(chunk == 0, sh[0], sp[0, 0])[:, :STATE].astype(f32)
    act_b = conv(bs, lagged(bs, prev_b, place.col, place.lags), ts[:, :STATE])
    keys = act_b * sigmoid(act_b)
    _, step, _, running, _ = steps_of(small, pick[...], hp[...])
    end = running[CHUNK - 1 : CHUNK]
    weight = jnp.exp(end - running) * place.open_end * step
    carried = widen(jnp.broadcast_to(jnp.exp(end) * place.unbroken, (8, 128)), spread[...])[0:1]
    memory = carried * carry[...] + dot(keys, values * widen(weight, spread[...]), 0, 0)
    total = fall[0:1] * carried
    carry[...] = memory
    fall[...] = jnp.broadcast_to(total, fall.shape)

    @pl.when(chunk == pl.num_programs(1) - 1)
    def _():
        pack(out, memory, total)


def scan_kernel(sequences, offs, x, xp, xh, s, sp, sh, tx, ts, hp, pick, spread, first, out, kept, carry):
    group, chunk = pl.program_id(0), pl.program_id(1)
    place = Place(offs, group, chunk, sequences)

    @pl.when(chunk == 0)
    def _():
        carry[...] = first[0]

    memory = carry[...]
    kept[0, 0] = memory
    small = rows_of(s)
    xs = rows_of(x).astype(f32)
    prev = jnp.where(chunk == 0, xh[0], xp[0, 0]).astype(f32)
    act = conv(xs, lagged(xs, prev, place.col, place.lags), tx[...])
    values = act * sigmoid(act)
    mix = small[:, :MIX].astype(f32)
    prev_m = jnp.where(chunk == 0, sh[0], sp[0, 0])[:, :MIX].astype(f32)
    act_m = conv(mix, lagged(mix, prev_m, place.col, place.lags), ts[...])
    act_m = act_m * sigmoid(act_m)
    keys, queries = act_m[:, :STATE], act_m[:, STATE:]
    _, step, _, running, lower = steps_of(small, pick[...], hp[...])
    end = running[CHUNK - 1 : CHUNK]
    inflow = jnp.exp(running) * place.fresh
    weight = jnp.exp(end - running) * place.open_end
    carried = jnp.exp(end) * place.unbroken
    wide = widen(
        jnp.concatenate([step, inflow, weight, jnp.broadcast_to(carried, (8, 128)), hp[...]], axis=0),
        spread[...],
    )
    step_w, inflow_w, weight_w = (wide[i * CHUNK : (i + 1) * CHUNK] for i in range(3))
    carried_w = wide[3 * CHUNK : 3 * CHUNK + 1]
    skip_w = wide[3 * CHUNK + 10 : 3 * CHUNK + 11]
    weighted = values * step_w
    within = (place.col == place.row) & (lower > 0.5)
    scores = dot(queries, keys, 1, 1)
    running_t = running.T
    left = lax.broadcasted_iota(jnp.int32, (1, 128), 1) < HEAD_DIM
    from_memory = dot(queries, memory) * inflow_w + skip_w * values
    for pair in range(values.shape[1] // 128):
        lanes = slice(128 * pair, 128 * pair + 128)
        mixed = []
        for h in (2 * pair, 2 * pair + 1):
            gaps = running[:, h : h + 1] - running_t[h : h + 1, :]
            mixed.append(scores * jnp.exp(jnp.where(within, gaps, -1e30)))
        part = weighted[:, lanes]
        both = jnp.concatenate([jnp.where(left, part, 0.0), jnp.where(left, 0.0, part)], axis=0)
        result = dot(jnp.concatenate(mixed, axis=1), both) + from_memory[:, lanes]
        out[:, 0, :, lanes] = result.astype(bf16).reshape(out.shape[0], out.shape[2], 128)
    carry[...] = carried_w * memory + dot(keys, weighted * weight_w, 0, 0)


def direct_kernel(sequences, offs, s, sp, sh, ts, hp, pick, spread, dy, out, carry, fall):
    group, chunk = pl.program_id(0), pl.program_id(1)
    place = Place(offs, group, chunk, sequences)

    @pl.when(chunk == 0)
    def _():
        carry[...] = jnp.zeros_like(carry)
        fall[...] = jnp.ones_like(fall)

    small = rows_of(s)
    cs = small[:, STATE:MIX].astype(f32)
    prev_c = jnp.where(chunk == 0, sh[0], sp[0, 0])[:, STATE:MIX].astype(f32)
    act_c = conv(cs, lagged(cs, prev_c, place.col, place.lags), ts[:, STATE:])
    queries = act_c * sigmoid(act_c)
    _, _, _, running, _ = steps_of(small, pick[...], hp[...])
    end = running[CHUNK - 1 : CHUNK]
    wide = widen(
        jnp.concatenate(
            [
                jnp.exp(running) * place.fresh,
                jnp.broadcast_to(jnp.exp(end) * place.unbroken, (8, 128)),
            ],
            axis=0,
        ),
        spread[...],
    )
    grad = rows_of(dy).astype(f32) * wide[:CHUNK]
    total = carry[...] + fall[0:1] * dot(queries, grad, 0, 0)
    carry[...] = total
    falls = fall[0:1] * wide[CHUNK : CHUNK + 1]
    fall[...] = jnp.broadcast_to(falls, fall.shape)

    @pl.when(chunk == pl.num_programs(1) - 1)
    def _():
        pack(out, total, falls)


def conv_back(du, ahead, taps, own_seg, ahead_segs):
    rows = du.shape[0]
    whole = jnp.concatenate([du, ahead], axis=0)
    total = taps[3:4] * du
    for lag in range(1, KW):
        keep = (own_seg == ahead_segs[lag - 1]).astype(f32)
        total = total + taps[3 - lag : 4 - lag] * (whole[lag : lag + rows] * keep)
    return total


def conv_rim(du, taps, seg):
    at = places(-EDGE, EDGE, 0)
    whole = jnp.concatenate([jnp.zeros((EDGE, du.shape[1]), f32), du[:EDGE]], axis=0)
    total = jnp.zeros((EDGE, du.shape[1]), f32)
    for lag in range(1, KW):
        keep = (seg(at) == seg(at + lag)).astype(f32)
        total = total + taps[3 - lag : 4 - lag] * (whole[lag : lag + EDGE] * keep)
    return total


def column_sums(du, current, lags):
    rows = [jnp.sum(du * lags[KW - 2 - k], axis=0, keepdims=True) for k in range(KW - 1)]
    rows.append(jnp.sum(du * current, axis=0, keepdims=True))
    rows.append(jnp.sum(du, axis=0, keepdims=True))
    return rows


def back_kernel(
    sequences, offs, x, xp, xh, s, sp, sh, tx, ts, hp, pick, spread, dy, kept, later,
    dx, tail, rim, gx, gs, gh, carry, next_x, next_s,
):
    group = pl.program_id(0)
    chunks = pl.num_programs(1)
    chunk = chunks - 1 - pl.program_id(1)
    place = Place(offs, group, chunk, sequences)
    seg = functools.partial(segment, offs, group, sequences=sequences)
    width = tx.shape[1]
    head_count = width // HEAD_DIM

    @pl.when(pl.program_id(1) == 0)
    def _():
        carry[...] = later[0]
        next_x[...] = jnp.zeros_like(next_x)
        next_s[...] = jnp.zeros_like(next_s)

    @pl.when((pl.program_id(1) == 0) & (group == 0))
    def _():
        gx[...] = jnp.zeros_like(gx)
        gs[...] = jnp.zeros_like(gs)
        gh[...] = jnp.zeros_like(gh)

    small = rows_of(s)
    xs = rows_of(x).astype(f32)
    prev = jnp.where(chunk == 0, xh[0], xp[0, 0]).astype(f32)
    lags_x = lagged(xs, prev, place.col, place.lags)
    act = conv(xs, lags_x, tx[...])
    gate = sigmoid(act)
    values = act * gate
    slope_x = gate * (1.0 + act * (1.0 - gate))
    mix = small[:, :MIX].astype(f32)
    prev_m = jnp.where(chunk == 0, sh[0], sp[0, 0])[:, :MIX].astype(f32)
    lags_m = lagged(mix, prev_m, place.col, place.lags)
    act_m = conv(mix, lags_m, ts[...])
    gate_m = sigmoid(act_m)
    keys, queries = (act_m * gate_m)[:, :STATE], (act_m * gate_m)[:, STATE:]
    slope_m = gate_m * (1.0 + act_m * (1.0 - gate_m))
    shifted, step, log_a, running, lower = steps_of(small, pick[...], hp[...])
    end = running[CHUNK - 1 : CHUNK]
    carried = jnp.exp(end) * place.unbroken
    wide = widen(
        jnp.concatenate(
            [
                step,
                jnp.exp(running) * place.fresh,
                jnp.exp(end - running) * place.open_end,
                jnp.broadcast_to(carried, (8, 128)),
                hp[...],
            ],
            axis=0,
        ),
        spread[...],
    )
    step_w, inflow_w, weight_w = (wide[i * CHUNK : (i + 1) * CHUNK] for i in range(3))
    carried_w = wide[3 * CHUNK : 3 * CHUNK + 1]
    skip_w = wide[3 * CHUNK + 10 : 3 * CHUNK + 11]
    grad = rows_of(dy).astype(f32)
    weighted = values * step_w
    memory = kept[0, 0]
    back = carry[...]

    scores = dot(queries, keys, 1, 1)
    running_t = running.T
    within = (place.col == place.row) & (lower > 0.5)
    left = lax.broadcasted_iota(jnp.int32, (1, 128), 1) < HEAD_DIM
    lane = lax.broadcasted_iota(jnp.int32, (1, 128), 1)

    grad_in = grad * inflow_w
    to_end = weighted * weight_w
    back_values = dot(keys, back) * weight_w
    from_state = weighted * back_values
    grad_run = grad_in * dot(queries, memory) - from_state
    grad_scores = jnp.zeros((CHUNK, CHUNK), f32)
    run_cols = jnp.zeros((CHUNK, 128), f32)
    run_rows = []
    back_weighted = []
    for pair in range(width // 128):
        lanes = slice(128 * pair, 128 * pair + 128)
        decays = []
        for h in (2 * pair, 2 * pair + 1):
            gaps = running[:, h : h + 1] - running_t[h : h + 1, :]
            decays.append(jnp.exp(jnp.where(within, gaps, -1e30)))
        decay = jnp.concatenate(decays, axis=0)
        mixed = jnp.concatenate([scores, scores], axis=0) * decay
        part = grad[:, lanes]
        both = jnp.concatenate([jnp.where(left, part, 0.0), jnp.where(left, 0.0, part)], axis=0)
        grad_mixed = dot(both, weighted[:, lanes], 1, 1)
        through = grad_mixed * decay
        grad_scores = grad_scores + through[:CHUNK] + through[CHUNK:]
        pull = grad_mixed * mixed
        sums = jnp.sum(pull, axis=1, keepdims=True)
        run_cols = run_cols + jnp.where(lane == 2 * pair, sums[:CHUNK], 0.0)
        run_cols = run_cols + jnp.where(lane == 2 * pair + 1, sums[CHUNK:], 0.0)
        run_rows.append(jnp.sum(pull[:CHUNK], axis=0, keepdims=True))
        run_rows.append(jnp.sum(pull[CHUNK:], axis=0, keepdims=True))
        back_weighted.append(dot(mixed, both, 0, 0) + back_values[:, lanes])
    back_weighted = jnp.concatenate(back_weighted, axis=1)
    run_rows.append(jnp.zeros((CHUNK - head_count, CHUNK), f32))
    run_cols = run_cols - jnp.concatenate(run_rows, axis=0).T

    grad_queries = dot(grad_scores, keys) + dot(grad_in, memory, 1, 1)
    grad_keys = dot(grad_scores, queries, 0, 0) + dot(to_end, back, 1, 1)
    end_sum = jnp.sum(from_state, axis=0, keepdims=True) + carried_w * jnp.sum(
        back * memory, axis=0, keepdims=True
    )
    carry[...] = carried_w * back + dot(queries, grad_in, 0, 0)

    sums = narrow(
        jnp.concatenate(
            [grad_run, back_weighted * values, jnp.broadcast_to(end_sum, (8, width))], axis=0
        ),
        spread[...],
    )
    grad_log = running_sum(lower, run_cols + sums[:CHUNK], 0) + sums[2 * CHUNK : 2 * CHUNK + 1]
    rate = -jnp.exp(hp[1:2])
    grad_step = (sums[CHUNK : 2 * CHUNK] + grad_log * rate) * sigmoid(shifted)
    gh[0:1] += jnp.sum(grad_step, axis=0, keepdims=True)
    gh[1:2] += jnp.sum(grad_log * log_a, axis=0, keepdims=True)

    du_x = (back_weighted * step_w + skip_w * grad) * slope_x
    du_m = jnp.concatenate([grad_keys, grad_queries], axis=1) * slope_m
    rows = column_sums(du_x, xs, lags_x)
    rows.append(jnp.sum(grad * values, axis=0, keepdims=True))
    rows.append(jnp.zeros((2, width), f32))
    gx[...] += jnp.concatenate(rows, axis=0)
    rows = column_sums(du_m, mix, lags_m)
    rows.append(jnp.zeros((3, MIX), f32))
    gs[...] += jnp.concatenate(rows, axis=0)

    grad_x = conv_back(du_x, next_x[...], tx[...], place.col, place.ahead)
    grad_m = conv_back(du_m, next_s[...], ts[...], place.col, place.ahead)
    next_x[...] = du_x[:8]
    next_s[...] = du_m[:8]
    shape = (dx.shape[0], dx.shape[2])
    dx[:, 0, :, :width] = grad_x.astype(bf16).reshape(shape + (width,))
    dx[:, 0, :, width : width + MIX] = grad_m.astype(bf16).reshape(shape + (MIX,))
    placed = dot(grad_step, pick[...], 1, 1)
    dx[:, 0, :, width + MIX :] = placed.astype(bf16).reshape(shape + (SMALL - MIX,))

    @pl.when(chunk == chunks - 1)
    def _():
        tail[0, :, :width] = grad_x[CHUNK - EDGE :]
        tail[0, :, width:] = grad_m[CHUNK - EDGE :]

    @pl.when(chunk == 0)
    def _():
        rim[0, :, :width] = conv_rim(du_x, tx[...], seg)
        rim[0, :, width:] = conv_rim(du_m, ts[...], seg)


def back_projection_kernel(gz, gx, wz, wx, ws, x, out, sums):
    width = wx.shape[1]
    grad = dot(gz[...], wz[...], 1, 1) + dot(gx[:, :width], wx[...], 1, 1)
    grad = grad + dot(gx[:, width:], ws[...], 1, 1)
    out[...] = grad.astype(bf16)
    rows = x[...].astype(f32)
    unit = rows * lax.rsqrt(jnp.mean(rows * rows, axis=1, keepdims=True) + EPS)
    partial = (grad * unit).reshape(-1, 8, D)

    @pl.when(pl.program_id(0) == 0)
    def _():
        sums[...] = jnp.zeros_like(sums)

    sums[...] += jnp.sum(partial, axis=0)


def back_projection(grads, weights, x_all, deps):
    tokens = x_all.shape[0]
    block = 256

    def rows(cols):
        return pl.BlockSpec((block, cols), lambda i: (i, 0))

    def kernel(*refs):
        back_projection_kernel(*refs[:6], *refs[6 + len(deps) :])

    return pl.pallas_call(
        kernel,
        grid=(tokens // block,),
        in_specs=[rows(grad.shape[1]) for grad in grads]
        + [pl.BlockSpec(w.shape, lambda i: (0, 0)) for w in weights]
        + [rows(D)]
        + [pl.BlockSpec(memory_space=pl.ANY)] * len(deps),
        out_specs=[rows(D), pl.BlockSpec((8, D), lambda i: (0, 0))],
        out_shape=[
            jax.ShapeDtypeStruct((tokens, D), bf16),
            jax.ShapeDtypeStruct((8, D), f32),
        ],
        compiler_params=pltpu.CompilerParams(
            dimension_semantics=("arbitrary",), vmem_limit_bytes=VMEM_LIMIT
        ),
        cost_estimate=cost(0),
    )(*grads, *weights, x_all, *deps)


def adam(weight, first, second, grad, rate):
    first_new = BETA_ONE * first + (1.0 - BETA_ONE) * grad
    second_new = BETA_TWO * second + (1.0 - BETA_TWO) * grad * grad
    update = (
        first_new
        / (1.0 - BETA_ONE**STEP)
        / (jnp.sqrt(second_new / (1.0 - BETA_TWO**STEP)) + ADAM_EPS)
    )
    return (weight - rate * (update + DECAY * weight), first_new, second_new)


def shifted_along(value, axis, by):
    peers = lax.axis_size(axis)
    pairs = [(i, i + by) for i in range(peers) if 0 <= i + by < peers]
    return lax.ppermute(value, axis, pairs)


def adam_kernel(last, refs):
    home, small, weight, first, second, *outs = refs
    cuts = range(0, home.shape[2], 128)
    grad = [home[k, :, cut : cut + 128] for cut in cuts for k in range(home.shape[0])]
    grad = jnp.concatenate(grad, axis=1).astype(f32)
    if last:
        extra = jnp.zeros((grad.shape[0], grad.shape[1] - SMALL), f32)
        extra = jnp.concatenate([small[...], extra], axis=1)
        grad = jnp.where(pl.program_id(0) == last, extra, grad)
    new = adam(weight[...], first[...], second[...], grad, rate_input)
    for out, value in zip(outs[-3:], new):
        out[...] = value


def adam_columns(state, home, small, start, done):
    senders, rows, width = home.shape
    steps = 4
    block = pl.BlockSpec((rows, senders * 128), lambda i: (0, start + i))

    def sent(i):
        i = jnp.minimum(i, steps - 1)
        return (lax.rem(i, 2), 0, lax.div(i, 2))

    specs = [pl.BlockSpec((senders // 2, rows, width // 2), sent)]
    args = [home]
    if small is not None:
        specs.append(pl.BlockSpec(small.shape, lambda i: (0, 0)))
        args.append(small)
    specs += [block] * 3
    args += state
    aliases = {}
    if done is not None:
        aliases = {len(args) + k: k for k in range(3)}
        specs += [pl.BlockSpec(memory_space=pl.ANY)] * 3
        args += done

    def kernel(*refs):
        refs = list(refs)
        if small is None:
            refs.insert(1, None)
        adam_kernel(0 if small is None else steps, refs)

    return pl.pallas_call(
        kernel,
        grid=(steps + (small is not None),),
        in_specs=specs,
        out_specs=[block] * 3,
        out_shape=[jax.ShapeDtypeStruct(part.shape, f32) for part in state],
        input_output_aliases=aliases,
        compiler_params=pltpu.CompilerParams(
            dimension_semantics=("arbitrary",), vmem_limit_bytes=VMEM_LIMIT
        ),
        cost_estimate=pl.CostEstimate(flops=0, bytes_accessed=1000, transcendentals=0),
    )(*args)


def halo_before(value):
    size = lax.axis_size("y")
    zh, y = lax.axis_index("zh"), lax.axis_index("y")
    near = lax.ppermute(value, "y", [(i, (i + 1) % size) for i in range(size)])
    far = lax.ppermute(value[1], ROW, [(size - 1, size)])
    wrapped = jnp.stack([far, near[0]])
    return jnp.where(y > 0, near, wrapped)


def halo_after(value):
    size = lax.axis_size("y")
    y = lax.axis_index("y")
    near = lax.ppermute(value, "y", [((i + 1) % size, i) for i in range(size)])
    far = lax.ppermute(value[0], ROW, [(size, size - 1)])
    wrapped = jnp.stack([near[1], far])
    return jnp.where(y < size - 1, near, wrapped)


def passed(value, reverse, first=(), second=(), started=None):
    size = lax.axis_size("y")
    zh, y = lax.axis_index("zh"), lax.axis_index("y")
    others = [value]
    for far in range(1, size):
        others.append(lax.ppermute(value, "y", [(i, (i + far) % size) for i in range(size)]))

    def fold(memory, order, found):
        for zl, at in order:
            found[zl] = jnp.where(y == at, memory, found[zl])
            packed = others[0][zl]
            for far in range(1, size):
                packed = jnp.where(lax.rem(y - at + size, size) == far, others[far][zl], packed)
            memory = carried_over(memory, packed)
        return memory

    order = [(zl, at) for zl in range(2) for at in range(size)]
    order = order[::-1] if reverse else order
    shape = value.shape[1:2] + (STATE,) + value.shape[3:]
    zeros = jnp.zeros(shape, f32)
    others[1] = after(others[1], *first)
    extra = started(others[1]) if started else None
    half = fold(zeros, order, [zeros, zeros]).astype(bf16)
    half = lax.ppermute(half, "zh", [(1, 0)] if reverse else [(0, 1)])
    half = after(half, *second, extra).astype(f32)
    found = [zeros, zeros]
    fold(half, order, found)
    return jnp.concatenate(found, axis=0), others[1], extra


def swapped(value, axis):
    return lax.ppermute(value, axis, [(0, 1), (1, 0)])


def is_square(axes):
    return [lax.axis_size(axis) for axis in axes] == [2] * len(axes)


def flip(axis):
    return lax.axis_index(axis), 1 - lax.axis_index(axis)


def gather_q(value, deps=(), deps_corner=()):
    from_x, from_z = swapped(value, "x"), swapped(value, "zl")
    from_z = after(from_z, *deps)
    corner = after(swapped(from_z, "x"), *deps_corner)
    z, x, core = (lax.axis_index(axis) for axis in Q)
    places, pieces = [], []
    for dz, dx, block in ((0, 0, value), (0, 1, from_x), (1, 0, from_z), (1, 1, corner)):
        place = ((z ^ dz) * 2 + (x ^ dx)) * 2
        for other in (0, 1):
            places.append(place + (core ^ other))
            pieces.append(swapped(block, "core") if other else block)
    return jnp.stack(places).astype(jnp.int32), pieces


def gather_row(value):
    from_y, from_z = swapped(value, "y"), swapped(value, "zh")
    corner = swapped(from_z, "y")
    zh, y = lax.axis_index("zh"), lax.axis_index("y")
    bits = [(zh ^ dz, y ^ dy) for dz in (0, 1) for dy in (0, 1)]
    return (bits, [value, from_y, from_z, corner]), (from_y, from_z)


def front_kernel(places, *refs):
    pieces, rows_of_w, gain = refs[:8], refs[8:12], refs[12]
    x_out, normed_out, small_out, w_out = refs[13:]
    step = pl.program_id(0)
    for k in range(8):

        @pl.when(step == k)
        def _(piece=pieces[k], w=rows_of_w[k // 2], part=k % 2):
            rows = piece[...]
            kept = x_out.shape[1]
            x_out[0] = rows[:kept]
            packed_rows(rows[kept:], small_out)
            rows = rows[:kept].astype(f32)
            inverse = lax.rsqrt(jnp.mean(rows * rows, axis=1, keepdims=True) + EPS)
            normed_out[0] = (rows * inverse * gain[...]).astype(bf16)
            size = w_out.shape[1]
            w_out[0] = w[part * size : part * size + size]


def front(tokens_gathered, w_gathered, gain, kept, row_count):
    spots, pieces = tokens_gathered
    bits, blocks = w_gathered
    w_spots = [(zh * 2 + zl) * 2 + y for zh, y in bits for zl in (0, 1)]
    places = jnp.stack([spots, jnp.stack(w_spots).astype(jnp.int32)])
    rows, cols = pieces[0].shape
    w_rows, width = blocks[0].shape
    shapes = [(8, kept, cols)] * 2 + [(8, row_count, D // 32, SMALL), (8, w_rows // 2, width)]

    def out_spec(shape, line):
        tail = (0,) * (len(shape) - 1)
        return pl.BlockSpec((1,) + shape[1:], lambda i, at: (at[line, i],) + tail)

    return pl.pallas_call(
        front_kernel,
        grid_spec=pltpu.PrefetchScalarGridSpec(
            num_scalar_prefetch=1,
            grid=(8,),
            in_specs=[pl.BlockSpec((rows, cols), lambda i, at: (0, 0))] * 8
            + [pl.BlockSpec((w_rows, width), lambda i, at: (0, 0))] * 4
            + [pl.BlockSpec((1, cols), lambda i, at: (0, 0))],
            out_specs=[out_spec(shape, k // 3) for k, shape in enumerate(shapes)],
        ),
        out_shape=[jax.ShapeDtypeStruct(shape, bf16) for shape in shapes],
        compiler_params=pltpu.CompilerParams(
            dimension_semantics=("arbitrary",), vmem_limit_bytes=VMEM_LIMIT
        ),
        cost_estimate=cost(0),
    )(places, *pieces, *blocks, gain[None])


def late_kernel(places, *refs):
    wz, wo, z_out, o_out = refs[:4], refs[4:8], refs[8], refs[9]
    for k in range(4):

        @pl.when(pl.program_id(0) == k)
        def _(z=wz[k], o=wo[k]):
            z_out[0, :, 0] = z[...].reshape(z_out.shape[1], z_out.shape[3], z_out.shape[4])
            o_out[0] = o[...]


def late(wz, wo, deps):
    bits, z_blocks = wz
    o_blocks = wo[1]
    places = jnp.stack([jnp.stack(pair) for pair in bits]).astype(jnp.int32)
    z_rows, z_cols = z_blocks[0].shape
    o_rows, o_cols = o_blocks[0].shape

    def kernel(places, *refs):
        late_kernel(places, *refs[:8], *refs[8 + len(deps) :])

    return pl.pallas_call(
        kernel,
        grid_spec=pltpu.PrefetchScalarGridSpec(
            num_scalar_prefetch=1,
            grid=(4,),
            in_specs=[pl.BlockSpec((z_rows, z_cols), lambda i, at: (0, 0))] * 4
            + [pl.BlockSpec((o_rows, o_cols), lambda i, at: (0, 0))] * 4
            + [pl.BlockSpec(memory_space=pl.ANY)] * len(deps),
            out_specs=[
                pl.BlockSpec(
                    (1, 2, 1, z_rows // 2, z_cols), lambda i, at: (at[i, 0], 0, at[i, 1], 0, 0)
                ),
                pl.BlockSpec((1, o_rows, o_cols), lambda i, at: (at[i, 0] * 2 + at[i, 1], 0, 0)),
            ],
        ),
        out_shape=[
            jax.ShapeDtypeStruct((2, 2, 2, z_rows // 2, z_cols), bf16),
            jax.ShapeDtypeStruct((4, o_rows, o_cols), bf16),
        ],
        compiler_params=pltpu.CompilerParams(
            dimension_semantics=("arbitrary",), vmem_limit_bytes=VMEM_LIMIT
        ),
        cost_estimate=cost(4),
    )(places, *z_blocks, *o_blocks, *deps)


def packed_rows(rows, out):
    across = rows.shape[1] // 128
    blocks, height = out.shape[1], out.shape[2]
    tile = 0
    for block in range(blocks):
        for row in range(0, height, 16):
            for lane in range(0, SMALL, 128):
                r, c = tile // across * 16, tile % across * 128
                out[0, block, row : row + 16, lane : lane + 128] = rows[r : r + 16, c : c + 128]
                tile += 1


def pack_rows(small):
    blocks, height, _ = small.shape
    tiles = small.reshape(blocks, height // 16, 16, SMALL // 128, 128)
    tiles = jnp.moveaxis(tiles, 3, 2).reshape(-1, D // 128, 16, 128)
    return jnp.moveaxis(tiles, 1, 2).reshape(-1, D)


def spread_sum(value, axes):
    parts = lax.all_to_all(value.astype(bf16), axes, split_axis=0, concat_axis=0, tiled=True)
    return jnp.sum(parts.astype(f32), axis=0)


def over_y(value):
    y, other = flip("y")
    value = value.astype(bf16)
    got = swapped(lax.dynamic_index_in_dim(value, other, 1, False), "y")
    return lax.dynamic_index_in_dim(value, y, 1, False).astype(f32) + got.astype(f32)


def over_z(value):
    zh, other = flip("zh")
    got = swapped(lax.dynamic_index_in_dim(value, other, 0, False).astype(bf16), "zh")
    return lax.dynamic_index_in_dim(value, zh, 0, False) + got.astype(f32)


def row_sum(value):
    if is_square(ROW):
        return over_z(over_y(value))
    return spread_sum(value.reshape((-1,) + value.shape[2:]), ROW)


def stacked(gathered):
    bits, blocks = gathered
    result = jnp.zeros((len(blocks),) + blocks[0].shape, blocks[0].dtype)
    for (zh, y), block in zip(bits, blocks):
        result = lax.dynamic_update_index_in_dim(result, block, zh * 2 + y, 0)
    return result


def after(value, *others, us=0):
    others = [other for other in others if other is not None]
    if not others and not us:
        return value
    anywhere = pl.BlockSpec(memory_space=pl.ANY)
    return pl.pallas_call(
        lambda *refs: None,
        in_specs=[anywhere] * (1 + len(others)),
        out_specs=anywhere,
        out_shape=jax.ShapeDtypeStruct(value.shape, value.dtype),
        input_output_aliases={0: 0},
        cost_estimate=cost(us),
    )(value, *others)


def carried_over(memory, packed):
    packed = packed.astype(f32)
    fall = jnp.sum(packed[:, STATE : STATE + 3], axis=1, keepdims=True)
    return fall * memory + packed[:, :STATE]


def three_parts(value):
    high = lax.reduce_precision(value, 8, 7)
    middle = lax.reduce_precision(value - high, 8, 7)
    low = value - high - middle
    return jnp.stack([high, middle, low]).astype(bf16)


def multiply(a, rights, on_a, block, deps=(), us=0):
    size = a.shape[1 - on_a]
    count = len(rights)

    def kernel(*refs):
        left = refs[0][...]
        outs = refs[1 + count + len(deps) :]
        for right, out in zip(refs[1 : 1 + count], outs):
            out[...] = dot(left, right[...], on_a, 0).astype(bf16)

    if on_a:
        left_spec = pl.BlockSpec((block, a.shape[1]), lambda i: (i, 0))
    else:
        left_spec = pl.BlockSpec((a.shape[0], block), lambda i: (0, i))
    return pl.pallas_call(
        kernel,
        grid=(size // block,),
        in_specs=[left_spec]
        + [pl.BlockSpec(right.shape, lambda i: (0, 0)) for right in rights]
        + [pl.BlockSpec(memory_space=pl.ANY)] * len(deps),
        out_specs=[pl.BlockSpec((block, right.shape[1]), lambda i: (i, 0)) for right in rights],
        out_shape=[jax.ShapeDtypeStruct((size, right.shape[1]), bf16) for right in rights],
        compiler_params=pltpu.CompilerParams(
            dimension_semantics=("arbitrary",), vmem_limit_bytes=VMEM_LIMIT
        ),
        cost_estimate=cost(us),
    )(a, *rights, *deps)


def product(a, b, on_a, on_b):
    return lax.dot_general(a, b, (((on_a,), (on_b,)), ((), ())), preferred_element_type=f32)


def local(
    x_in, lengths, cotangent, w_in, m_in, v_in, w_out, m_out, v_out, conv_w, m_conv, v_conv,
    vectors, m_vec, v_vec, head_params, m_head, v_head,
):
    row_shape = (lax.axis_size("zh"), lax.axis_size("y"))
    row_count = row_shape[0] * row_shape[1]
    head_size = lax.axis_size("x") * lax.axis_size("core")
    q_shape = (lax.axis_size("zl"), head_size)
    qn = q_shape[0] * head_size
    devices = row_count * qn
    q = lax.axis_index(Q)
    groups, own, _ = x_in.shape
    sequences = lengths.shape[1]
    span = own * head_size
    runs = q_shape[0] * groups
    chunks = span // CHUNK
    part = CHUNK // own
    tokens = groups * own * qn
    width = INNER // qn
    heads_own = HEADS // qn
    unit = INNER // devices
    square = is_square(ROW + Q)
    strided = unit % HEAD_DIM == 0
    rows_in = D // devices
    conv_rows, vec_rows, head_cols = conv_w.shape[0], vectors.shape[0], head_params.shape[1]
    full_shape = (row_shape[0], q_shape[0], row_shape[1], head_size)

    def split(array, size):
        lead = array.shape[:-1]
        n = len(lead)
        if strided:
            array = array.reshape(lead + full_shape + (size // devices,))
            order = (n + 1, n + 3) + tuple(range(n)) + (n, n + 2, n + 4)
            array = array.transpose(order)
        else:
            array = jnp.moveaxis(array.reshape(lead + (qn, size // qn)), -2, 0)
        return array.reshape((qn,) + lead + (size // qn,))

    def join(array, size):
        lead = array.shape[1:-1]
        n = len(lead)
        if strided:
            array = array.reshape(q_shape + lead + row_shape + (size // devices,))
            order = tuple(range(2, 2 + n)) + (2 + n, 0, 3 + n, 1, 4 + n)
            array = array.transpose(order)
        else:
            array = jnp.moveaxis(array, 0, -2)
        return array.reshape(lead + (size,))

    def own_of(array, size):
        return lax.dynamic_index_in_dim(split(array, size), q, 0, False)

    def by_rows(array):
        array = array.reshape(row_shape + q_shape + array.shape[2:])
        return jnp.swapaxes(array, 1, 2)

    own_heads = own_of(jnp.arange(HEADS, dtype=jnp.int32), HEADS)

    payload = jnp.concatenate(
        [
            conv_w.astype(bf16).T.reshape(-1),
            vectors.astype(bf16),
            three_parts(head_params).reshape(-1),
        ]
    )
    payload = jnp.pad(payload, (0, rows_in * HEADS - payload.shape[0])).reshape(rows_in, HEADS)
    small_own = jnp.concatenate([w_in[:, 2 * INNER :].astype(bf16), payload], axis=1)
    if square:
        small_row = stacked(gather_row(small_own)[0])
    else:
        small_row = lax.all_gather(small_own, ROW, axis=0, tiled=False)
    payload_rows = small_row[:, :, SMALL - HEADS :].reshape(1, -1, width)
    payload_rows = jnp.broadcast_to(payload_rows, (qn,) + payload_rows.shape[1:])
    both = [split(w_in[:, first : first + INNER].astype(bf16), INNER) for first in (INNER, 0)]
    both = jnp.concatenate(both + [payload_rows], axis=1)
    both = lax.all_to_all(both, Q, split_axis=0, concat_axis=0, tiled=True)
    payload = both[:, 2 * rows_in :].reshape(q_shape + row_shape + (rows_in * HEADS,))
    payload = payload.transpose(2, 0, 3, 1, 4).reshape(devices, -1)
    w_x_own, w_z_own = both[:, :rows_in], both[:, rows_in : 2 * rows_in]
    w_out_b = w_out.astype(bf16)
    if square:
        w_x, hops_x = gather_row(w_x_own.reshape(-1, width))
        w_z, hops_z = gather_row(after(w_z_own.reshape(-1, width), *hops_x))
        w_o, hops_o = gather_row(after(w_out_b, *hops_z))
    else:
        hops_z, hops_o = (), ()
        w_x, w_z = (lax.all_gather(w, ROW, axis=0, tiled=False) for w in (w_x_own, w_z_own))
        w_x, w_z = (by_rows(w).reshape(D, width) for w in (w_x, w_z))
        w_o = lax.all_gather(w_out_b, ALL, axis=0, tiled=True)
        w_o = lax.dynamic_slice_in_dim(w_o, q * width, width, 0)
    cut = [conv_rows * KW, vec_rows, 9 * head_cols]
    taps = jnp.moveaxis(payload[:, : cut[0]].reshape(devices, KW, conv_rows), 0, 1)
    taps = taps.reshape(KW, CONV).astype(f32)
    vec = payload[:, cut[0] : cut[0] + cut[1]].reshape(-1).astype(f32)
    params = payload[:head_size, cut[0] + cut[1] : sum(cut)].astype(f32)
    params = jnp.sum(params.reshape(head_size, 3, 3, head_cols), axis=1)
    params = jnp.moveaxis(params, 0, 1).reshape(3, HEADS)
    norm_gain = vec[:D]
    conv_bias = vec[D : D + CONV]
    gate_gain = own_of(vec[D + CONV :], INNER)
    table = jnp.concatenate([taps, conv_bias[None], jnp.zeros((3, CONV), f32)], axis=0)
    taps_x = own_of(table[:, :INNER], INNER)
    taps_s = table[:, INNER:]
    lanes = jnp.arange(128, dtype=jnp.int32)
    head_of_lane = jnp.pad(own_heads, (0, 128 - heads_own), constant_values=-1)
    pick = (lanes[:, None] == head_of_lane[None, :]).astype(bf16)
    hp = jnp.sum(
        jnp.where(jnp.arange(HEADS)[:, None] == head_of_lane[None, :], params[:, :, None], 0.0), 1
    )
    hp = jnp.pad(hp, ((0, 5), (0, 0)))
    spread = (lanes[:, None] == jnp.arange(width)[None, :] // HEAD_DIM).astype(bf16)
    spread = jnp.concatenate([spread, spread], axis=0)
    starts = jnp.arange(q_shape[0]) + lax.axis_index("zh") * q_shape[0]
    starts = (starts * row_shape[1] + lax.axis_index("y")) * span
    offsets = jnp.cumsum(lengths, axis=1) - lengths
    offsets = offsets[None] - starts[:, None, None]
    offsets = offsets.reshape(runs, sequences).astype(jnp.int32)

    x_flat = x_in.reshape(groups * own, D)
    if square:
        joined = after(jnp.concatenate([x_flat, pack_rows(small_row)], axis=0), both)
        x_all, normed, w_small, w_x = front(
            gather_q(joined, hops_x + (norm_gain,), w_x[1][3:]), w_x, norm_gain, groups * own, row_count
        )
        w_x = w_x.reshape(D, width)
        x_all, normed = x_all.reshape(tokens, D), normed.reshape(tokens, D)
        w_small = jnp.swapaxes(w_small, 0, 1)
    else:
        x_all = lax.all_gather(x_flat, Q, axis=0, tiled=True)
        w_small = lax.all_gather(small_own, ROW + Q, axis=0, tiled=False)
        w_small = w_small.reshape(row_count, qn, rows_in, SMALL)
    w_small = by_rows(w_small).reshape(D, SMALL)
    if not square:
        x_float = x_all.astype(f32)
        scale = lax.rsqrt(jnp.mean(x_float * x_float, axis=-1, keepdims=True) + EPS)
        normed = (x_float * scale * norm_gain).astype(bf16)
    token_shape = (qn, groups, own)
    x_raw, s_raw = multiply(normed, (w_x, w_small), 1, 256)
    x_raw = x_raw.reshape(token_shape + (width,))
    s_raw = s_raw.reshape(token_shape + (SMALL,))

    def last_rows(raw):
        raw = raw.reshape(q_shape + raw.shape[1:])
        return raw[:, head_size - 1, :, own - EDGE :]

    halo = halo_before(jnp.concatenate([last_rows(x_raw), last_rows(s_raw)], axis=-1))
    halo = halo.reshape(runs, EDGE, width + SMALL)
    x_halo, s_halo = halo[..., :width], halo[..., width:]

    def at(reverse):
        return (lambda i: chunks - 1 - i) if reverse else (lambda i: i)

    def token_spec(cols, reverse):
        def place(g, i):
            return (lax.div(g, groups) * chunks + at(reverse)(i), lax.rem(g, groups), 0, 0)

        return pl.BlockSpec((part, 1, own, cols), place)

    def before_spec(cols, reverse):
        def place(g, i):
            block = lax.div(g, groups) * head_size + part * at(reverse)(i) - 1
            return (jnp.maximum(block, 0), lax.rem(g, groups), own // EDGE - 1, 0)

        return pl.BlockSpec((1, 1, EDGE, cols), place)

    def group_spec(*dims):
        return pl.BlockSpec((1,) + dims, lambda g, i: (g,) + (0,) * len(dims))

    def whole_spec(*dims):
        return pl.BlockSpec(dims, lambda g, i: (0,) * len(dims))

    def kept_spec(reverse):
        return pl.BlockSpec((1, 1, STATE, width), lambda g, i: (g, at(reverse)(i), 0, 0))

    offs_spec = pl.BlockSpec(memory_space=pltpu.SMEM)

    def x_specs(reverse):
        return [token_spec(width, reverse), before_spec(width, reverse), group_spec(EDGE, width)]

    def s_specs(reverse):
        return [token_spec(SMALL, reverse), before_spec(SMALL, reverse), group_spec(EDGE, SMALL)]

    head_specs = [whole_spec(8, 128), whole_spec(128, 128), whole_spec(256, width)]
    x_args = (x_raw, x_raw, x_halo)
    s_args = (s_raw, s_raw, s_halo)
    head_args = (hp, pick, spread)
    state_ref = pltpu.VMEM((STATE, width), f32)
    fall_ref = pltpu.VMEM((8, width), f32)

    def call(kernel, us, in_specs, out_specs, out_shape, scratch, deps=()):
        count = len(in_specs)
        anywhere = [pl.BlockSpec(memory_space=pl.ANY)] * len(deps)

        def body(*refs):
            kernel(sequences, *refs[:count], *refs[count + len(deps) :])

        call = pl.pallas_call(
            body,
            grid=(runs, chunks),
            in_specs=in_specs + anywhere,
            out_specs=out_specs,
            out_shape=out_shape,
            scratch_shapes=scratch,
            compiler_params=pltpu.CompilerParams(
                dimension_semantics=("arbitrary", "arbitrary"), vmem_limit_bytes=VMEM_LIMIT
            ),
            cost_estimate=cost(us),
        )
        return lambda *args: call(*args, *deps)

    with jax.named_scope("memory_own"):
        ended = call(
            state_kernel, 0,
            [offs_spec] + x_specs(False) + s_specs(False)
            + [whole_spec(8, width), whole_spec(8, MIX)] + head_specs,
            group_spec(STATE + EDGE, width),
            jax.ShapeDtypeStruct((runs, STATE + EDGE, width), bf16),
            [state_ref, fall_ref],
        )(offsets, *x_args, *s_args, taps_x, taps_s, *head_args)
    cot_flat = after(cotangent.reshape(groups * own, D), x_all)
    cot_all = lax.all_gather(cot_flat, Q, axis=0, tiled=False).reshape(tokens, D)
    ended = ended.reshape(q_shape[0], groups, STATE + EDGE, width)
    incoming, _, _ = passed(ended, False, hops_z)

    with jax.named_scope("scan"):
        scanned, kept = call(
            scan_kernel, 0,
            [offs_spec] + x_specs(False) + s_specs(False)
            + [whole_spec(8, width), whole_spec(8, MIX)] + head_specs + [group_spec(STATE, width)],
            [token_spec(width, False), kept_spec(False)],
            [
                jax.ShapeDtypeStruct(token_shape + (width,), bf16),
                jax.ShapeDtypeStruct((runs, chunks, STATE, width), f32),
            ],
            [state_ref],
        )(offsets, *x_args, *s_args, taps_x, taps_s, *head_args, incoming)

    if square:
        w_z, w_o = late(w_z, w_o, (scanned,))
        w_z, w_o = w_z.reshape(D, width), w_o.reshape(width, D)
    gate_in = product(normed, w_z, 1, 0)
    grad_gnorm = product(cot_all, w_o, 1, 1)
    scan_b = scanned.reshape(tokens, width).astype(f32)
    gate_sig = jax.nn.sigmoid(gate_in)
    gate = gate_in * gate_sig
    gated = scan_b * gate
    grad_gain_in = grad_gnorm * gate_gain
    sums = jnp.stack([jnp.sum(gated * gated, axis=1), jnp.sum(grad_gain_in * gated, axis=1)])
    sums = lax.psum(sums, Q) / INNER
    inverse = lax.rsqrt(sums[0] + EPS)[:, None]
    gated_unit = gated * inverse
    gnorm = (gated_unit * gate_gain).astype(bf16)
    grad_gate_gain = jnp.sum(grad_gnorm * gated_unit, axis=0)
    grad_gated = inverse * (grad_gain_in - gated * (inverse * inverse * sums[1][:, None]))
    grad_scan = (grad_gated * gate).astype(bf16).reshape(token_shape + (width,))
    slope = gate_sig * (1.0 + gate_in * (1.0 - gate_sig))
    grad_z = (grad_gated * scan_b * slope).astype(bf16)

    with jax.named_scope("memory_back"):
        direct = call(
            direct_kernel, 8,
            [offs_spec] + s_specs(False) + [whole_spec(8, MIX)] + head_specs
            + [token_spec(width, False)],
            group_spec(STATE + EDGE, width),
            jax.ShapeDtypeStruct((runs, STATE + EDGE, width), bf16),
            [state_ref, fall_ref],
        )(offsets, *s_args, taps_s, *head_args, grad_scan)
    grad_out = multiply(gnorm, (cot_all,), 0, 128, (direct,))[0]
    branch = multiply(gnorm, (w_o,), 1, 256, (direct,))[0].reshape(qn, groups, own, D)
    own_z = multiply(normed, (grad_z,), 0, 256, (direct,))[0]
    def sum_out(met):
        value = after(grad_out, met)
        if square:
            return over_y(value.reshape(row_shape + (unit, D)))
        if strided:
            return row_sum(value.reshape(row_shape + (unit, D)))
        full = jnp.zeros((INNER, D), bf16)
        full = lax.dynamic_update_slice_in_dim(full, value, q * width, 0)
        return spread_sum(full.reshape(devices, unit, D), ALL)

    later, met, half_out = passed(
        direct.reshape(q_shape[0], groups, STATE + EDGE, width),
        True,
        (grad_out, own_z),
        (branch,),
        sum_out,
    )
    own_z = after(own_z, met)
    branch = after(branch, later)
    branch = lax.psum_scatter(branch, Q, scatter_dimension=0, tiled=False)
    result = (x_in.astype(f32) + branch.astype(f32)).astype(bf16)
    grad_out = over_z(half_out) if square else half_out

    def line_blocks(grad):
        cols = grad.shape[1]
        grad = grad.reshape(row_shape[0], q_shape[0], row_shape[1], head_size * rows_in, cols)
        if square:
            return over_y(jnp.swapaxes(grad, 1, 2))
        return row_sum(jnp.swapaxes(grad, 1, 2)).reshape(qn, rows_in, cols)

    def line_rest(early, *deps):
        early = after(early, *deps)
        return (over_z(early) if square else early).reshape(qn, rows_in, early.shape[-1])

    def home(grad):
        return lax.all_to_all(grad.astype(bf16), Q, split_axis=0, concat_axis=0, tiled=True)

    early_z = line_blocks(own_z)
    home_z = home(line_rest(early_z))

    with jax.named_scope("scan_back"):
        dx, tail, rim, gx, gs, gh = call(
            back_kernel, 22,
            [offs_spec] + x_specs(True) + s_specs(True)
            + [whole_spec(8, width), whole_spec(8, MIX)] + head_specs
            + [token_spec(width, True), kept_spec(True), group_spec(STATE, width)],
            [
                token_spec(width + SMALL, True),
                group_spec(EDGE, width + MIX), group_spec(EDGE, width + MIX),
                whole_spec(8, width), whole_spec(8, MIX), whole_spec(8, 128),
            ],
            [
                jax.ShapeDtypeStruct(token_shape + (width + SMALL,), bf16),
                jax.ShapeDtypeStruct((runs, EDGE, width + MIX), f32),
                jax.ShapeDtypeStruct((runs, EDGE, width + MIX), f32),
                jax.ShapeDtypeStruct((8, width), f32),
                jax.ShapeDtypeStruct((8, MIX), f32),
                jax.ShapeDtypeStruct((8, 128), f32),
            ],
            [state_ref, pltpu.VMEM((8, width), f32), pltpu.VMEM((8, MIX), f32)],
            (half_out,),
        )(offsets, *x_args, *s_args, taps_x, taps_s, *head_args, grad_scan, kept, later)
    tail = tail.reshape(q_shape[0], groups, EDGE, width + MIX)
    rim = halo_after(after(rim, early_z, grad_out).reshape(q_shape[0], groups, EDGE, width + MIX))
    tail = (tail + rim).astype(bf16)
    for zl in range(q_shape[0]):
        last = (zl + 1) * head_size - 1
        dx = dx.at[last, :, own - EDGE :, : width + MIX].set(tail[zl])
    grad_x = dx.reshape(tokens, width + SMALL)

    own_x = multiply(normed, (grad_x,), 0, 256)[0]
    early_x = line_blocks(own_x[:, :width])
    own_s = own_x[:, width:].reshape(full_shape + (rows_in, SMALL)).transpose(1, 3, 0, 2, 4, 5)
    own_s = spread_sum(own_s.reshape(qn, row_count, rows_in, SMALL), Q)
    home_s = row_sum(own_s.reshape(row_shape + (rows_in, SMALL)))
    grad_normed, gain_sums = back_projection(
        (grad_z, grad_x), (w_z, w_x, w_small), x_all, (branch, own_x)
    )
    grad_own = lax.psum_scatter(
        grad_normed.reshape(qn, groups, own, D), Q, scatter_dimension=0, tiled=False
    ).astype(f32)

    grad_norm_gain = jnp.sum(gain_sums, axis=0)
    x_own = x_in.astype(f32)
    inverse = lax.rsqrt(jnp.mean(x_own * x_own, axis=-1, keepdims=True) + EPS)
    grad_unit = grad_own * norm_gain
    pulled = jnp.mean(grad_unit * x_own, axis=-1, keepdims=True)
    grad_x_own = inverse * (grad_unit - x_own * (inverse * inverse * pulled))
    input_grad = (grad_x_own + cotangent.astype(f32)).astype(bf16)

    def place_own(array, size):
        mine = (jnp.arange(qn) == q).astype(f32).reshape((qn,) + (1,) * array.ndim)
        return join(array[None] * mine, size)

    table = jnp.concatenate([place_own(gx[:5], INNER), gs[:5]], axis=1)
    grad_vec = jnp.concatenate([grad_norm_gain, table[4], place_own(grad_gate_gain, INNER)])
    grad_skip = jnp.sum(gx[5].reshape(heads_own, HEAD_DIM), axis=1)
    grad_heads = jnp.concatenate([gh[:2, :heads_own], grad_skip[None]], axis=0)
    grad_heads = place_own(grad_heads, HEADS).reshape(3, head_size, head_cols)
    grad_heads = jnp.moveaxis(grad_heads, 1, 0).reshape(1, head_size, 3 * head_cols)
    grad_heads = jnp.broadcast_to(grad_heads, (devices // head_size,) + grad_heads.shape[1:])
    packed = jnp.concatenate(
        [
            jnp.moveaxis(table[:4].reshape(KW, devices, conv_rows), 1, 0).reshape(devices, -1),
            grad_vec.reshape(devices, vec_rows),
            grad_heads.reshape(devices, -1),
        ],
        axis=1,
    )
    used = packed.shape[1]
    packed = jnp.pad(packed, ((0, 0), (0, -used % 1024))).reshape(devices, -1, 128)
    packed = lax.all_to_all(packed, ALL, split_axis=0, concat_axis=0, tiled=True)
    packed = jnp.sum(packed, axis=0).reshape(-1)
    grad_conv = packed[: conv_rows * KW].reshape(KW, conv_rows).T
    grad_vec = packed[conv_rows * KW : conv_rows * KW + vec_rows]
    grad_head = packed[conv_rows * KW + vec_rows : used].reshape(3, head_cols)

    home_x = home(line_rest(early_x, grad_normed))
    if square:
        in_new = adam_columns((w_in, m_in, v_in), home_z, None, 0, None)
        in_new = adam_columns((w_in, m_in, v_in), home_x, home_s, 4, in_new)
    else:
        grad_in = [join(home_z, INNER).astype(f32), join(home_x, INNER).astype(f32)]
        grad_in = jnp.concatenate(grad_in + [home_s[:, : MIX + HEADS]], axis=1)
        in_new = adam(w_in, m_in, v_in, grad_in, rate_input)
    out_new = adam(w_out, m_out, v_out, grad_out.astype(f32), rate_output)
    conv_new = adam(conv_w, m_conv, v_conv, grad_conv, rate_conv)
    vec_new = adam(vectors, m_vec, v_vec, grad_vec, rate_vector)
    head_new = adam(head_params, m_head, v_head, grad_head, rate_head)
    return (result, input_grad, *in_new, *out_new, *conv_new, *vec_new, *head_new)


def solution(mesh):
    seq, head = mesh.shape["seq"], mesh.shape["head"]
    fine = Mesh(mesh.devices.reshape(2, 2, seq // 4, head // 2, 2), ALL)
    token, row = P(None, ALL, None), P(ALL, None)
    line, heads = P(ALL), P(None, ("x", "core"))
    return jax.shard_map(
        local,
        mesh=fine,
        in_specs=(token, P(), token) + (row,) * 9 + (line,) * 3 + (heads,) * 3,
        out_specs=(token, token) + (row,) * 9 + (line,) * 3 + (heads,) * 3,
        check_vma=False,
    )
```
